128 devices in a mesh: wide: 16 (over x, y_lo, core), narrow: 8 (over z, y_hi).
Axes of the slice: x: 4, y: 4 (y_hi: 2, y_lo: 2; y = y_hi * 2 + y_lo), z: 4, core: 2. Of those that a mesh axis runs over, the one named last changes fastest.
Arguments:
- node_features: bfloat16 [8192, 25, 128], P(('wide', 'narrow')), may hold values from -6 to 6
- frames: bfloat16 [8192, 48, 165], P(('wide', 'narrow')), may hold values from -6 to 6
- radial: bfloat16 [8192, 48, 128], P(('wide', 'narrow')), may hold values from 0.29882812 to 3
- neighbours: int32 [8192, 48], P(('wide', 'narrow')), may hold values from 0 to 8191, as said below
- counts: int32 [8192], P(('wide', 'narrow')), may hold values from 16 to 48
- coefficients: float32 [32], P('wide'), may hold values from 0.05 to 0.5
- w_zero: bfloat16 [32, 640, 640], P('wide'), may hold values from -0.25 to 0.25
- w_one: bfloat16 [32, 2, 512, 512], P('wide'), may hold values from -0.1875 to 0.1875
- w_two: bfloat16 [32, 2, 384, 384], P('wide'), may hold values from -0.21875 to 0.21875
- w_three: bfloat16 [32, 2, 256, 256], P('wide'), may hold values from -0.25 to 0.25
- w_four: bfloat16 [32, 2, 128, 128], P('wide'), may hold values from -0.375 to 0.375
Outputs:
- conv_out: float32 [8192, 25, 128], P(('wide', 'narrow'))
The draws below stay inside these ranges and needn't reach their ends.
Inputs may be any that keep to these rules, and one draw needn't show every extreme that they name: `neighbours`: each neighbour of an atom lies in the atom's own aligned block of 64 atoms or in one of the two cyclically adjacent blocks. `counts`: slots at or beyond an atom's count are padding and carry arbitrary indices.
All inputs are finite; a program needn't handle non-finite values.
Results may differ from the reference program's by a relative error of at most 0.02.
Values may be sent and summed in bfloat16 or wider, within the bound.
No kernel may reach another device: no remote copies, remote signals or barrier semaphores. Data moves between devices by JAX's collectives and lax.ppermute only.
A program may use at most 192 MiB of HBM per device.

```python
import math
import jax
import jax.numpy as jnp
from jax import lax

C = 128
EXPERTS = 32
NEIGH = 48
ATOM_DEV = 64
ATOMS = 8192
N_WIDE = 16


def draw_neighbours(key, part):
    block_count = ATOMS // ATOM_DEV
    side_key, position_key = jax.random.split(jax.random.fold_in(key, 11))
    home_block = (jnp.arange(ATOMS, dtype=jnp.int32) // ATOM_DEV)[:, None]
    offset_step = jax.random.randint(side_key, (ATOMS, NEIGH), -1, 2)
    position = jax.random.randint(position_key, (ATOMS, NEIGH), 0, ATOM_DEV)
    return ((home_block + offset_step + block_count) % block_count * ATOM_DEV + position).astype(jnp.int32)


def with_ends(values, rng, low, high):
    dims = values.shape
    index_at = [jax.random.randint(jax.random.fold_in(rng, axis), (), 0, dims[axis]) for axis in range(len(dims))]
    values = values.at[tuple(index_at)].set(low)
    longest = dims.index(max(dims))
    index_at[longest] = (index_at[longest] + 1) % dims[longest]
    return values.at[tuple(index_at)].set(high)


def block_levels(own_key, shape, cuts, least, top_value):
    factor_of = 1.0
    for dim, parts in cuts:
        steps = jax.random.uniform(jax.random.fold_in(jax.random.fold_in(own_key, 6), dim), (parts,), jnp.float32, least / len(cuts), top_value / len(cuts))
        factor_of = factor_of * jnp.repeat(jnp.exp(steps), shape[dim] // parts).reshape((-1,) + (1,) * (len(shape) - 1 - dim))
    return factor_of


def noise(own_key, dims, spread, most, cuts=(), kind=jnp.bfloat16):
    factor_of = block_levels(own_key, dims, cuts, -0.22, 0.18) if cuts else 1.0
    array = jax.random.normal(own_key, dims, jnp.float32) * spread * factor_of
    return jnp.minimum(jnp.maximum(array, -most), most).astype(kind)


def setup_inputs(seed: int = 0) -> dict:
    key_list = jax.random.split(jax.random.key(seed), 12)
    return {
        "node_features": noise(key_list[0], (ATOMS, 25, C), 1.0, 6.0, ((0, 128),)),
        "frames": noise(key_list[1], (ATOMS, NEIGH, 165), 0.45, 6.0, ((0, 128),)),
        "radial": jnp.clip(jnp.exp(math.log(3.0) - 2.306499 * jax.random.uniform(key_list[2], (ATOMS, NEIGH, C), jnp.float32) ** block_levels(key_list[2], (ATOMS, NEIGH, C), ((0, 128),), -0.2, 0.2)), 0.29882812, 3.0).astype(jnp.bfloat16),
        "neighbours": draw_neighbours(jax.random.fold_in(key_list[11], 71), 0),
        "counts": with_ends(jax.random.randint(key_list[4], (ATOMS,), NEIGH // 3, NEIGH + 1), jax.random.fold_in(key_list[4], 1), NEIGH // 3, NEIGH).astype(jnp.int32),
        "coefficients": jnp.clip(jnp.exp(math.log(0.5) - 2.3025851 * jax.random.uniform(key_list[5], (EXPERTS,), jnp.float32) ** block_levels(key_list[5], (EXPERTS,), ((0, 16),), -0.2, 0.2)), 0.05, 0.5),
        "w_zero": noise(key_list[6], (EXPERTS, 5 * C, 5 * C), (5 * C) ** -0.5, 0.25, ((0, 16),)),
        "w_one": noise(key_list[7], (EXPERTS, 2, 4 * C, 4 * C), (8 * C) ** -0.5, 0.1875, ((0, 16),)),
        "w_two": noise(key_list[8], (EXPERTS, 2, 3 * C, 3 * C), (6 * C) ** -0.5, 0.21875, ((0, 16),)),
        "w_three": noise(key_list[9], (EXPERTS, 2, 2 * C, 2 * C), (4 * C) ** -0.5, 0.25, ((0, 16),)),
        "w_four": noise(key_list[10], (EXPERTS, 2, C, C), (2 * C) ** -0.5, 0.375, ((0, 16),)),
    }


def rotate(frames, features, inverse):
    pieces = []
    offset = 0
    for degree in range(5):
        order_size = 2 * degree + 1
        frame_block = frames[:, offset:offset + order_size * order_size].reshape(-1, order_size, order_size).astype(jnp.float32)
        component = features[:, degree * degree:degree * degree + order_size, :].astype(jnp.float32)
        if inverse:
            pieces.append(jnp.einsum('rji,rjc->ric', frame_block, component, precision=lax.Precision.HIGHEST))
        else:
            pieces.append(jnp.einsum('rij,rjc->ric', frame_block, component, precision=lax.Precision.HIGHEST))
        offset += order_size * order_size
    return jnp.concatenate(pieces, axis=1)

def convolve(rotated, merged):
    row_count = rotated.shape[0]
    channels = rotated.shape[2]
    outputs = [None] * 25
    central = jnp.stack([rotated[:, degree * degree + degree] for degree in range(5)], axis=1).reshape(row_count, 5 * channels)
    result = jnp.dot(central, merged[0], preferred_element_type=jnp.float32).reshape(row_count, 5, channels)
    for degree in range(5):
        outputs[degree * degree + degree] = result[:, degree]
    for order in range(1, 5):
        kept = 5 - order
        plus = jnp.stack([rotated[:, degree * degree + degree + order] for degree in range(order, 5)], axis=1).reshape(row_count, kept * channels)
        minus = jnp.stack([rotated[:, degree * degree + degree - order] for degree in range(order, 5)], axis=1).reshape(row_count, kept * channels)
        stacked = jnp.concatenate([plus, minus], axis=0)
        weight_pair = merged[order]
        real_part = jnp.dot(stacked, weight_pair[0], preferred_element_type=jnp.float32)
        imag_part = jnp.dot(stacked, weight_pair[1], preferred_element_type=jnp.float32)
        out_plus = (real_part[:row_count] - imag_part[row_count:]).reshape(row_count, kept, channels)
        out_minus = (real_part[row_count:] + imag_part[:row_count]).reshape(row_count, kept, channels)
        for column, degree in enumerate(range(order, 5)):
            outputs[degree * degree + degree + order] = out_plus[:, column]
            outputs[degree * degree + degree - order] = out_minus[:, column]
    return jnp.stack(outputs, axis=1)

def messages(gathered, frames, radial, merged):
    rotated = (rotate(frames, gathered, False) * radial.astype(jnp.float32)[:, None, :]).astype(jnp.bfloat16)
    mixed = convolve(rotated, merged)
    scalar = mixed[:, 0:1, :]
    gated = jnp.concatenate([jax.nn.silu(scalar), mixed[:, 1:, :] * jax.nn.sigmoid(scalar)], axis=1)
    return rotate(frames, gated, True)

def merge_weights(coefficients, weights):
    grouped_coeff = coefficients.reshape(N_WIDE, -1)
    grouped = weights.astype(jnp.float32).reshape((N_WIDE, grouped_coeff.shape[1]) + weights.shape[1:])
    partials = jnp.einsum('ge,ge...->g...', grouped_coeff, grouped, precision=lax.Precision.HIGHEST).astype(jnp.bfloat16)
    partials = lax.optimization_barrier(partials)
    return lax.optimization_barrier(jnp.sum(partials.astype(jnp.float32), axis=0)).astype(jnp.bfloat16)

def reference(node_features, frames, radial, neighbours, counts, coefficients, w_zero, w_one, w_two, w_three, w_four):
    merged = tuple((merge_weights(coefficients, weights) for weights in (w_zero, w_one, w_two, w_three, w_four)))
    atoms_total = node_features.shape[0]
    channels = node_features.shape[2]
    block_count = atoms_total // ATOM_DEV
    live_slots = (lax.broadcasted_iota(jnp.int32, neighbours.shape, 1) < counts[:, None]).astype(jnp.float32)

    def one_block(inputs):
        index_block, frame_block, radial_block, live_block = inputs
        gathered = jnp.take(node_features, index_block.reshape(-1), axis=0)
        result = messages(gathered, frame_block.reshape(-1, 165), radial_block.reshape(-1, channels), merged)
        result = result.reshape(ATOM_DEV, NEIGH, 25, channels)
        return lax.optimization_barrier(jnp.sum(result * live_block[:, :, None, None], axis=1))
    summed = lax.map(one_block, (neighbours.reshape(block_count, ATOM_DEV, NEIGH), frames.reshape(block_count, ATOM_DEV, NEIGH, 165), radial.reshape(block_count, ATOM_DEV, NEIGH, channels), live_slots.reshape(block_count, ATOM_DEV, NEIGH)))
    summed = summed.reshape(atoms_total, 25, channels)
    return summed / jnp.sqrt(counts.astype(jnp.float32))[:, None, None]
```

```python
import functools

import jax
import jax.numpy as jnp
import numpy as np
from jax import lax
from jax.experimental import pallas as pl
from jax.experimental.pallas import tpu as pltpu
from jax.sharding import Mesh, PartitionSpec as P

WIDE = ("x", "yl", "core")
NARROW = ("z", "yh")
ATOM_AXES = WIDE + NARROW
SAME_CORE = ("z", "yh", "x", "yl")
C = 128
TILE = 256
WINDOW = 1024
BLOCKS_EACH = 11
FRAME_LANES = 256
INDEX_LANE = 165
DEPTH = (5, 8, 6, 4, 2)
START = (0, 5, 13, 19, 23)
VMEM = 100 * 2**20 // 2


def grouped_place():
    place = {}
    at = 0
    for degree in range(5):
        place[degree * degree + degree] = at
        at += 1
    for order in range(1, 5):
        for sign in (1, -1):
            for degree in range(order, 5):
                place[degree * degree + degree + sign * order] = at
                at += 1
    return place


PLACE = grouped_place()


def block_list():
    blocks = [(0, 0, o, i) for o in range(5) for i in range(5)]
    for order in range(1, 5):
        kept = 5 - order
        blocks += [(order, part, o, i) for part in range(2) for o in range(kept) for i in range(kept)]
    return blocks


BLOCKS = block_list()


def combine_kernel(table, coeff, w0, w1, w2, w3, w4, out, buf, sems):
    arrays = (w0, w1, w2, w3, w4)
    for j in range(BLOCKS_EACH):
        kind = table[j, 0]
        part = table[j, 1]
        row = pl.multiple_of(table[j, 3] * C, C)
        column = pl.multiple_of(table[j, 2] * C, C)
        for a, ref in enumerate(arrays):

            @pl.when(kind == a)
            def _():
                if a == 0:
                    source = ref.at[:, pl.ds(row, C), pl.ds(column, C)]
                else:
                    source = ref.at[:, part, pl.ds(row, C), pl.ds(column, C)]
                pltpu.make_async_copy(source, buf.at[j], sems.at[j]).start()

    for j in range(BLOCKS_EACH):
        pltpu.make_async_copy(w0.at[:, pl.ds(0, C), pl.ds(0, C)], buf.at[j], sems.at[j]).wait()
        total = coeff[0] * buf[j, 0].astype(jnp.float32) + coeff[1] * buf[j, 1].astype(jnp.float32)
        turned = total.T.astype(jnp.bfloat16)
        out[0, 64 * j : 64 * j + 64] = turned[:64]
        out[1, 64 * j : 64 * j + 64] = turned[64:]


def combine(table, coeff, weights):
    return pl.pallas_call(
        combine_kernel,
        grid_spec=pltpu.PrefetchScalarGridSpec(
            num_scalar_prefetch=2,
            grid=(1,),
            in_specs=[pl.BlockSpec(memory_space=pl.ANY)] * 5,
            out_specs=pl.BlockSpec((2, 64 * BLOCKS_EACH, C), lambda i, *_: (0, 0, 0)),
            scratch_shapes=[
                pltpu.VMEM((BLOCKS_EACH, 2, C, C), jnp.bfloat16),
                pltpu.SemaphoreType.DMA((BLOCKS_EACH,)),
            ],
        ),
        out_shape=jax.ShapeDtypeStruct((2, 64 * BLOCKS_EACH, C), jnp.bfloat16),
        compiler_params=pltpu.CompilerParams(vmem_limit_bytes=16 * 2**20),
        cost_estimate=pl.CostEstimate(flops=BLOCKS_EACH * C * C * 4, bytes_accessed=BLOCKS_EACH * C * C * 6, transcendentals=0),
        name="merge_group",
    )(table, coeff, *weights)


def spread_frames(turned, spread):
    for k in range(INDEX_LANE):
        spread[k] = jnp.broadcast_to(turned[k : k + 1, :], (16, TILE)).astype(jnp.bfloat16)


def tree_sum(terms):
    while len(terms) > 1:
        terms = [terms[i] + terms[i + 1] if i + 1 < len(terms) else terms[i] for i in range(0, len(terms), 2)]
    return terms[0]


def rotate_kernel(first, tiles, position, frames, radial, own, low, high, out, out_frames, table, gathered, spread):
    step = pl.program_id(0)

    @pl.when(step == 0)
    def _():
        for q in range(25):
            rows = jnp.concatenate([own[q], low[q], high[q]], axis=0)
            table[q * C : (q + 1) * C, :] = rows.T

    @pl.when(step < tiles[0])
    def _():
        rotate_tile(step, first, position, frames, radial, out, out_frames, table, gathered, spread)


def rotate_tile(step, first, position, frames, radial, out, out_frames, table, gathered, spread):
    begin = first[step]
    edge = lax.broadcasted_iota(jnp.int32, (TILE, C), 0) + step * TILE
    chosen = jnp.concatenate(
        [(position[begin + j] == edge).astype(jnp.float32).astype(jnp.bfloat16) for j in range(WINDOW // C)], axis=1
    )
    window = pl.ds(pl.multiple_of(begin * C, C), WINDOW)
    packed = jnp.dot(chosen, frames[window, :], preferred_element_type=jnp.float32)
    turned = packed.T
    out_frames[0] = turned[:168]
    weights = jnp.dot(chosen, radial[window, :], preferred_element_type=jnp.float32).T
    spread_frames(turned, spread)
    index = turned[INDEX_LANE : INDEX_LANE + 1, :].astype(jnp.int32)
    one_hot = (lax.broadcasted_iota(jnp.int32, (192, TILE), 0) == index).astype(jnp.float32).astype(jnp.bfloat16)
    for q in range(25):
        rows = slice(q * C, (q + 1) * C)
        got = jnp.dot(table[rows, :], one_hot, preferred_element_type=jnp.float32)
        gathered[rows, :] = (got * weights).astype(jnp.bfloat16)

    def channels(chunk, carried):
        at = chunk * 16
        offset = 0
        for degree in range(5):
            size = 2 * degree + 1
            base = degree * degree
            x = [gathered[pl.ds(pl.multiple_of((base + q) * C + at, 16), 16), :] for q in range(size)]
            for p in range(size):
                total = tree_sum([spread[offset + p * size + q] * x[q] for q in range(size)])
                out[0, pl.ds(pl.multiple_of(PLACE[base + p] * C + at, 16), 16), :] = total
            offset += size * size
        return carried

    lax.fori_loop(0, 8, channels, 0)


def rotate(tiles, first, position, frames, radial, own, low, high):
    whole = lambda *shape: pl.BlockSpec(shape, lambda i, *_: (0,) * len(shape))
    most = frames.shape[0] // TILE
    return pl.pallas_call(
        rotate_kernel,
        grid_spec=pltpu.PrefetchScalarGridSpec(
            num_scalar_prefetch=2,
            grid=(most,),
            in_specs=[
                whole(*position.shape),
                whole(*frames.shape),
                whole(*radial.shape),
                whole(*own.shape),
                whole(*own.shape),
                whole(*own.shape),
            ],
            out_specs=[
                pl.BlockSpec((1, 25 * C, TILE), lambda i, f, n: (jnp.minimum(i, n[0] - 1), 0, 0)),
                pl.BlockSpec((1, 168, TILE), lambda i, f, n: (jnp.minimum(i, n[0] - 1), 0, 0)),
            ],
            scratch_shapes=[
                pltpu.VMEM((25 * C, 192), jnp.bfloat16),
                pltpu.VMEM((25 * C, TILE), jnp.bfloat16),
                pltpu.VMEM((INDEX_LANE, 16, TILE), jnp.bfloat16),
            ],
        ),
        out_shape=[
            jax.ShapeDtypeStruct((most, 25 * C, TILE), jnp.bfloat16),
            jax.ShapeDtypeStruct((most, 168, TILE), jnp.float32),
        ],
        compiler_params=pltpu.CompilerParams(vmem_limit_bytes=VMEM),
        cost_estimate=pl.CostEstimate(flops=10**10, bytes_accessed=40 * 10**6, transcendentals=0),
        name="gather_rotate",
    )(first, tiles, position, frames, radial, own, low, high)


def place_weights(core, mine, other, mixes):
    for g, (order, part, o, i) in enumerate(BLOCKS):
        kept = C * DEPTH[order] // 2
        for half, ref in ((core, mine), (1 - core, other)):
            piece = ref[64 * g : 64 * g + 64, :]
            shift = half * 64

            def put(row, column, value):
                mixes[order][pl.ds(pl.multiple_of(row + shift, 64), 64), column : column + C] = value

            if order == 0:
                put(o * C, i * C, piece)
            elif part == 0:
                put(o * C, i * C, piece)
                put(kept + o * C, kept + i * C, piece)
            else:
                put(kept + o * C, i * C, piece)
                put(o * C, kept + i * C, -piece)


def mix_kernel(info, mine, other, rotated, frames, atoms, scale, out, m0, m1, m2, m3, m4, gated, message, spread, total):
    step = pl.program_id(0)
    mixes = (m0, m1, m2, m3, m4)

    @pl.when(step == 0)
    def _():
        place_weights(info[0], mine, other, mixes)
        total[...] = jnp.zeros_like(total)

    @pl.when(step < info[1])
    def _():
        mix_tile(rotated, frames, atoms, mixes, gated, message, spread, total)

    @pl.when(step == pl.num_programs(0) - 1)
    def _():
        for q in range(25):
            out[:, q, :] = total[q] * scale[...]


def mix_tile(rotated, frames, atoms, mixes, gated, message, spread, total):
    first = jnp.dot(mixes[0][...], rotated[0, : 5 * C], preferred_element_type=jnp.float32)
    scalar = first[:C]
    gate = 1.0 / (1.0 + jnp.exp(-scalar))
    for k in range(5):
        gated[k * C : (k + 1) * C] = (first[k * C : (k + 1) * C] * gate).astype(jnp.bfloat16)
    for order in range(1, 5):
        begin = START[order] * C
        size = DEPTH[order]
        mixed = jnp.dot(mixes[order][...], rotated[0, begin : begin + size * C], preferred_element_type=jnp.float32)
        for k in range(size):
            gated[begin + k * C : begin + (k + 1) * C] = (mixed[k * C : (k + 1) * C] * gate).astype(jnp.bfloat16)

    spread_frames(frames[0], spread)

    def channels(chunk, carried):
        at = chunk * 16
        offset = 0
        for degree in range(5):
            size = 2 * degree + 1
            base = degree * degree
            g = [gated[pl.ds(pl.multiple_of(PLACE[base + p] * C + at, 16), 16), :] for p in range(size)]
            for q in range(size):
                value = tree_sum([spread[offset + p * size + q] * g[p] for p in range(size)])
                message[pl.ds(pl.multiple_of((base + q) * C + at, 16), 16), :] = value
            offset += size * size
        return carried

    lax.fori_loop(0, 8, channels, 0)

    owner = (lax.broadcasted_iota(jnp.int32, (64, TILE), 0) == atoms[0]).astype(jnp.float32).astype(jnp.bfloat16)
    for q in range(25):
        total[q] += lax.dot_general(
            owner, message[q * C : (q + 1) * C, :], (((1,), (1,)), ((), ())), preferred_element_type=jnp.float32
        )


def mix(info, mine, other, rotated, frames, atoms, scale):
    whole = lambda *shape: pl.BlockSpec(shape, lambda i, *_: (0,) * len(shape))
    block = lambda a: pl.BlockSpec((1,) + a.shape[1:], lambda i, n: (jnp.minimum(i, n[1] - 1), 0, 0))
    return pl.pallas_call(
        mix_kernel,
        grid_spec=pltpu.PrefetchScalarGridSpec(
            num_scalar_prefetch=1,
            grid=(rotated.shape[0],),
            in_specs=[
                whole(*mine.shape),
                whole(*other.shape),
                block(rotated),
                block(frames),
                block(atoms),
                whole(*scale.shape),
            ],
            out_specs=whole(64, 25, C),
            scratch_shapes=[pltpu.VMEM((d * C, d * C), jnp.bfloat16) for d in DEPTH]
            + [
                pltpu.VMEM((25 * C, TILE), jnp.bfloat16),
                pltpu.VMEM((25 * C, TILE), jnp.bfloat16),
                pltpu.VMEM((INDEX_LANE, 16, TILE), jnp.bfloat16),
                pltpu.VMEM((25, 64, C), jnp.float32),
            ],
        ),
        out_shape=jax.ShapeDtypeStruct((64, 25, C), jnp.float32),
        compiler_params=pltpu.CompilerParams(vmem_limit_bytes=VMEM),
        cost_estimate=pl.CostEstimate(flops=15 * 10**9, bytes_accessed=40 * 10**6, transcendentals=10**6),
        name="mix_messages",
    )(info, mine, other, rotated, frames, atoms, scale)


def body(sizes, node_features, frames, radial, neighbours, counts, coefficients, *weights):
    atoms_here, _, channels = node_features.shape
    slots = neighbours.shape[1]
    edges = atoms_here * slots
    most = edges // TILE
    devices = int(np.prod(list(sizes.values())))
    n_narrow = sizes["z"] * sizes["yh"]
    n_xy = sizes["x"] * sizes["yl"]

    narrow = lax.axis_index(NARROW)
    rows = np.array([BLOCKS[min(g, len(BLOCKS) - 1)] for g in range(n_narrow * BLOCKS_EACH)], np.int32)
    table = lax.dynamic_slice_in_dim(jnp.asarray(rows), narrow * BLOCKS_EACH, BLOCKS_EACH, 0)
    partial = combine(table, coefficients, weights)
    share_rows = partial.shape[1] // n_xy
    parts = lax.all_to_all(partial.reshape(-1, share_rows, C), ("core", "x", "yl"), 0, 0, tiled=True)
    share = jnp.sum(parts.astype(jnp.float32), axis=0).astype(jnp.bfloat16)
    copies = jnp.broadcast_to(share[None], (n_narrow * n_xy,) + share.shape)
    mine = lax.all_to_all(copies, SAME_CORE, 0, 0, tiled=True).reshape(-1, C)
    other = lax.ppermute(mine, "core", [(0, 1), (1, 0)])

    own = node_features.transpose(1, 0, 2)
    up = [(i, (i + 1) % devices) for i in range(devices)]
    low = lax.ppermute(own, ATOM_AXES, up)
    high = lax.ppermute(own, ATOM_AXES, [(b, a) for a, b in up])

    block = lax.axis_index(ATOM_AXES)
    side = (neighbours // atoms_here - block) % devices
    local = neighbours % atoms_here + jnp.where(side == 0, 0, jnp.where(side == 1, 2 * atoms_here, atoms_here))
    before = np.tril(np.ones((atoms_here, atoms_here), np.int32), -1)
    offset = jnp.sum(before * counts[None, :], axis=1)
    ends = offset + counts
    slot = lax.broadcasted_iota(jnp.int32, (atoms_here, slots), 1)
    position = jnp.where(slot < counts[:, None], offset[:, None] + slot, -1).reshape(edges // C, 1, C)
    places = jnp.arange(edges, dtype=jnp.int32)
    atoms = jnp.sum((ends[None, :] <= places[:, None]).astype(jnp.int32), axis=1)
    starts = jnp.arange(most, dtype=jnp.int32) * TILE
    first_atom = jnp.sum((ends[None, :] <= starts[:, None]).astype(jnp.int32), axis=1)
    first = jnp.minimum(first_atom * slots // C, (edges - WINDOW) // C)
    tiles = ((jnp.sum(counts) + TILE - 1) // TILE).astype(jnp.int32).reshape(1)

    filled = jnp.concatenate(
        [
            frames.reshape(edges, -1),
            local.reshape(edges, 1).astype(jnp.bfloat16),
            jnp.zeros((edges, FRAME_LANES - INDEX_LANE - 1), jnp.bfloat16),
        ],
        axis=1,
    )
    rotated, turned = rotate(tiles, first, position, filled, radial.reshape(edges, C), own, low, high)
    scale = jnp.broadcast_to(1.0 / jnp.sqrt(counts.astype(jnp.float32))[:, None], (atoms_here, C))
    info = jnp.concatenate([lax.axis_index("core").astype(jnp.int32).reshape(1), tiles])
    return mix(info, mine, other, rotated, turned, atoms.reshape(most, 1, TILE), scale)


def solution(mesh):
    sizes = {"x": mesh.shape["wide"] // 4, "yl": 2, "core": 2, "z": mesh.shape["narrow"] // 2, "yh": 2}
    fine = Mesh(mesh.devices.reshape(tuple(sizes.values())), tuple(sizes))
    in_specs = (
        P(ATOM_AXES, None, None),
        P(ATOM_AXES, None, None),
        P(ATOM_AXES, None, None),
        P(ATOM_AXES, None),
        P(ATOM_AXES),
        P(WIDE),
        P(WIDE, None, None),
        P(WIDE, None, None, None),
        P(WIDE, None, None, None),
        P(WIDE, None, None, None),
        P(WIDE, None, None, None),
    )
    out_specs = P(ATOM_AXES, None, None)
    return jax.shard_map(functools.partial(body, sizes), mesh=fine, in_specs=in_specs, out_specs=out_specs, check_vma=False)
```

```python
import functools

import jax
import jax.numpy as jnp
import numpy as np
from jax import lax
from jax.experimental import pallas as pl
from jax.experimental.pallas import tpu as pltpu
from jax.sharding import Mesh, PartitionSpec as P

WIDE = ("x", "yl", "core")
NARROW = ("z", "yh")
ATOM_AXES = WIDE + NARROW
SAME_CORE = ("z", "yh", "x", "yl")
C = 128
TILE = 256
WINDOW = 1024
BLOCKS_EACH = 11
INDEX_LANE = 165
DEPTH = (5, 8, 6, 4, 2)
START = (0, 5, 13, 19, 23)
VMEM = 100 * 2**20 // 2


def grouped_place():
    place = {}
    at = 0
    for degree in range(5):
        place[degree * degree + degree] = at
        at += 1
    for order in range(1, 5):
        for sign in (1, -1):
            for degree in range(order, 5):
                place[degree * degree + degree + sign * order] = at
                at += 1
    return place


PLACE = grouped_place()


def block_list():
    blocks = [(0, 0, o, i) for o in range(5) for i in range(5)]
    for order in range(1, 5):
        kept = 5 - order
        blocks += [(order, part, o, i) for part in range(2) for o in range(kept) for i in range(kept)]
    return blocks


BLOCKS = block_list()


def combine_kernel(table, coeff, w0, w1, w2, w3, w4, out, buf, sems):
    arrays = (w0, w1, w2, w3, w4)
    for j in range(BLOCKS_EACH):
        kind = table[j, 0]
        part = table[j, 1]
        row = pl.multiple_of(table[j, 3] * C, C)
        column = pl.multiple_of(table[j, 2] * C, C)
        for a, ref in enumerate(arrays):

            @pl.when(kind == a)
            def _():
                if a == 0:
                    source = ref.at[:, pl.ds(row, C), pl.ds(column, C)]
                else:
                    source = ref.at[:, part, pl.ds(row, C), pl.ds(column, C)]
                pltpu.make_async_copy(source, buf.at[j], sems.at[j]).start()

    for j in range(BLOCKS_EACH):
        pltpu.make_async_copy(w0.at[:, pl.ds(0, C), pl.ds(0, C)], buf.at[j], sems.at[j]).wait()
        total = coeff[0] * buf[j, 0].astype(jnp.float32) + coeff[1] * buf[j, 1].astype(jnp.float32)
        turned = total.T.astype(jnp.bfloat16)
        out[0, 64 * j : 64 * j + 64] = turned[:64]
        out[1, 64 * j : 64 * j + 64] = turned[64:]


def combine(table, coeff, weights):
    return pl.pallas_call(
        combine_kernel,
        grid_spec=pltpu.PrefetchScalarGridSpec(
            num_scalar_prefetch=2,
            grid=(1,),
            in_specs=[pl.BlockSpec(memory_space=pltpu.HBM)] * 5,
            out_specs=pl.BlockSpec((2, 64 * BLOCKS_EACH, C), lambda i, *_: (0, 0, 0)),
            scratch_shapes=[
                pltpu.VMEM((BLOCKS_EACH, 2, C, C), jnp.bfloat16),
                pltpu.SemaphoreType.DMA((BLOCKS_EACH,)),
            ],
        ),
        out_shape=jax.ShapeDtypeStruct((2, 64 * BLOCKS_EACH, C), jnp.bfloat16),
        compiler_params=pltpu.CompilerParams(vmem_limit_bytes=62 * 2**20),
        cost_estimate=pl.CostEstimate(flops=BLOCKS_EACH * C * C * 4, bytes_accessed=BLOCKS_EACH * C * C * 6, transcendentals=0),
        name="merge_group",
    )(table, coeff, *weights)


def spread_frames(turned, spread):
    for k in range(INDEX_LANE):
        spread[k] = jnp.broadcast_to(turned[k : k + 1, :], (16, TILE)).astype(jnp.bfloat16)


def tree_sum(terms):
    while len(terms) > 1:
        terms = [terms[i] + terms[i + 1] if i + 1 < len(terms) else terms[i] for i in range(0, len(terms), 2)]
    return terms[0]


def compact_kernel(first, tiles, position, local, frames, radial, out_frames, out_radial):
    step = pl.program_id(0)

    @pl.when(step < tiles[0])
    def _():
        begin = first[step]
        edge = lax.broadcasted_iota(jnp.int32, (TILE, C), 0) + step * TILE
        chosen = jnp.concatenate(
            [(position[begin + j] == edge).astype(jnp.float32).astype(jnp.bfloat16) for j in range(WINDOW // C)], axis=1
        )
        window = pl.ds(pl.multiple_of(begin * C, C), WINDOW)
        packed = jnp.dot(chosen, frames[window, :], preferred_element_type=jnp.float32)
        out_frames[0, :INDEX_LANE] = packed.T
        index = jnp.concatenate([local[begin + j] for j in range(WINDOW // C)], axis=1)
        index = jnp.broadcast_to(index, (8, WINDOW)).astype(jnp.bfloat16)
        moved = lax.dot_general(index, chosen, (((1,), (1,)), ((), ())), preferred_element_type=jnp.float32)
        out_frames[0, INDEX_LANE : INDEX_LANE + 1] = moved[:1]
        out_radial[0] = jnp.dot(chosen, radial[window, :], preferred_element_type=jnp.float32).T


def compact(tiles, first, position, local, frames, radial):
    whole = lambda *shape: pl.BlockSpec(shape, lambda i, *_: (0,) * len(shape))
    most = frames.shape[0] // TILE
    tile = lambda rows: pl.BlockSpec((1, rows, TILE), lambda i, f, n: (jnp.minimum(i, n[0] - 1), 0, 0))
    return pl.pallas_call(
        compact_kernel,
        grid_spec=pltpu.PrefetchScalarGridSpec(
            num_scalar_prefetch=2,
            grid=(most,),
            in_specs=[whole(*a.shape) for a in (position, local, frames, radial)],
            out_specs=[tile(168), tile(C)],
        ),
        out_shape=[
            jax.ShapeDtypeStruct((most, 168, TILE), jnp.float32),
            jax.ShapeDtypeStruct((most, C, TILE), jnp.float32),
        ],
        compiler_params=pltpu.CompilerParams(vmem_limit_bytes=VMEM),
        cost_estimate=pl.CostEstimate(flops=2 * 10**10, bytes_accessed=40 * 10**6, transcendentals=0),
        name="compact_edges",
    )(first, tiles, position, local, frames, radial)


def rotate_kernel(tiles, frames, radial, own, low, high, out, table, gathered, spread):
    step = pl.program_id(0)

    @pl.when(step == 0)
    def _():
        for q in range(25):
            rows = jnp.concatenate([own[q], low[q], high[q]], axis=0)
            table[q * C : (q + 1) * C, :] = rows.T

    @pl.when(step < tiles[0])
    def _():
        rotate_tile(frames, radial, out, table, gathered, spread)


def rotate_tile(frames, radial, out, table, gathered, spread):
    spread_frames(frames[0], spread)
    index = frames[0, INDEX_LANE : INDEX_LANE + 1, :].astype(jnp.int32)
    one_hot = (lax.broadcasted_iota(jnp.int32, (192, TILE), 0) == index).astype(jnp.float32).astype(jnp.bfloat16)
    for q in range(25):
        rows = slice(q * C, (q + 1) * C)
        got = jnp.dot(table[rows, :], one_hot, preferred_element_type=jnp.float32)
        gathered[rows, :] = (got * radial[0]).astype(jnp.bfloat16)

    def channels(chunk, carried):
        at = chunk * 16
        offset = 0
        for degree in range(5):
            size = 2 * degree + 1
            base = degree * degree
            x = [gathered[pl.ds(pl.multiple_of((base + q) * C + at, 16), 16), :] for q in range(size)]
            for p in range(size):
                total = tree_sum([spread[offset + p * size + q] * x[q] for q in range(size)])
                out[0, pl.ds(pl.multiple_of(PLACE[base + p] * C + at, 16), 16), :] = total
            offset += size * size
        return carried

    lax.fori_loop(0, 8, channels, 0)


def rotate(tiles, frames, radial, own, low, high):
    whole = lambda *shape: pl.BlockSpec(shape, lambda i, *_: (0,) * len(shape))
    most = frames.shape[0]
    tile = lambda rows: pl.BlockSpec((1, rows, TILE), lambda i, n: (jnp.minimum(i, n[0] - 1), 0, 0))
    return pl.pallas_call(
        rotate_kernel,
        grid_spec=pltpu.PrefetchScalarGridSpec(
            num_scalar_prefetch=1,
            grid=(most,),
            in_specs=[tile(168), tile(C)] + [whole(*own.shape)] * 3,
            out_specs=tile(25 * C),
            scratch_shapes=[
                pltpu.VMEM((25 * C, 192), jnp.bfloat16),
                pltpu.VMEM((25 * C, TILE), jnp.bfloat16),
                pltpu.VMEM((INDEX_LANE, 16, TILE), jnp.bfloat16),
            ],
        ),
        out_shape=jax.ShapeDtypeStruct((most, 25 * C, TILE), jnp.bfloat16),
        compiler_params=pltpu.CompilerParams(vmem_limit_bytes=VMEM),
        cost_estimate=pl.CostEstimate(flops=10**10, bytes_accessed=40 * 10**6, transcendentals=0),
        name="gather_rotate",
    )(tiles, frames, radial, own, low, high)


def place_weights(core, mine, other, mixes):
    for g, (order, part, o, i) in enumerate(BLOCKS):
        kept = C * DEPTH[order] // 2
        for half, ref in ((core, mine), (1 - core, other)):
            piece = ref[64 * g : 64 * g + 64, :]
            shift = half * 64

            def put(row, column, value):
                mixes[order][pl.ds(pl.multiple_of(row + shift, 64), 64), column : column + C] = value

            if order == 0:
                put(o * C, i * C, piece)
            elif part == 0:
                put(o * C, i * C, piece)
                put(kept + o * C, kept + i * C, piece)
            else:
                put(kept + o * C, i * C, piece)
                put(o * C, kept + i * C, -piece)


def mix_kernel(info, mine, other, rotated, frames, atoms, scale, out, m0, m1, m2, m3, m4, gated, message, spread, total):
    step = pl.program_id(0)
    mixes = (m0, m1, m2, m3, m4)

    @pl.when(step == 0)
    def _():
        place_weights(info[0], mine, other, mixes)
        total[...] = jnp.zeros_like(total)

    @pl.when(step < info[1])
    def _():
        mix_tile(rotated, frames, atoms, mixes, gated, message, spread, total)

    @pl.when(step == pl.num_programs(0) - 1)
    def _():
        for q in range(25):
            out[q] = total[q] * scale[...]


def mix_tile(rotated, frames, atoms, mixes, gated, message, spread, total):
    first = jnp.dot(mixes[0][...], rotated[0, : 5 * C], preferred_element_type=jnp.float32)
    scalar = first[:C]
    gate = 1.0 / (1.0 + jnp.exp(-scalar))
    for k in range(5):
        gated[k * C : (k + 1) * C] = (first[k * C : (k + 1) * C] * gate).astype(jnp.bfloat16)
    for order in range(1, 5):
        begin = START[order] * C
        size = DEPTH[order]
        mixed = jnp.dot(mixes[order][...], rotated[0, begin : begin + size * C], preferred_element_type=jnp.float32)
        for k in range(size):
            gated[begin + k * C : begin + (k + 1) * C] = (mixed[k * C : (k + 1) * C] * gate).astype(jnp.bfloat16)

    spread_frames(frames[0], spread)

    def channels(chunk, carried):
        at = chunk * 16
        offset = 0
        for degree in range(5):
            size = 2 * degree + 1
            base = degree * degree
            g = [gated[pl.ds(pl.multiple_of(PLACE[base + p] * C + at, 16), 16), :] for p in range(size)]
            for q in range(size):
                value = tree_sum([spread[offset + p * size + q] * g[p] for p in range(size)])
                message[pl.ds(pl.multiple_of((base + q) * C + at, 16), 16), :] = value
            offset += size * size
        return carried

    lax.fori_loop(0, 8, channels, 0)

    owner = (lax.broadcasted_iota(jnp.int32, (64, TILE), 0) == atoms[0]).astype(jnp.float32).astype(jnp.bfloat16)
    for q in range(25):
        total[q] += lax.dot_general(
            owner, message[q * C : (q + 1) * C, :], (((1,), (1,)), ((), ())), preferred_element_type=jnp.float32
        )


def mix(info, mine, other, rotated, frames, atoms, scale):
    whole = lambda *shape: pl.BlockSpec(shape, lambda i, *_: (0,) * len(shape))
    block = lambda a: pl.BlockSpec((1,) + a.shape[1:], lambda i, n: (jnp.minimum(i, n[1] - 1), 0, 0))
    return pl.pallas_call(
        mix_kernel,
        grid_spec=pltpu.PrefetchScalarGridSpec(
            num_scalar_prefetch=1,
            grid=(rotated.shape[0],),
            in_specs=[
                whole(*mine.shape),
                whole(*other.shape),
                block(rotated),
                block(frames),
                block(atoms),
                whole(*scale.shape),
            ],
            out_specs=whole(25, 64, C),
            scratch_shapes=[pltpu.VMEM((d * C, d * C), jnp.bfloat16) for d in DEPTH]
            + [
                pltpu.VMEM((25 * C, TILE), jnp.bfloat16),
                pltpu.VMEM((25 * C, TILE), jnp.bfloat16),
                pltpu.VMEM((INDEX_LANE, 16, TILE), jnp.bfloat16),
                pltpu.VMEM((25, 64, C), jnp.float32),
            ],
        ),
        out_shape=jax.ShapeDtypeStruct((25, 64, C), jnp.float32),
        compiler_params=pltpu.CompilerParams(vmem_limit_bytes=VMEM),
        cost_estimate=pl.CostEstimate(flops=15 * 10**9, bytes_accessed=40 * 10**6, transcendentals=10**6),
        name="mix_messages",
    )(info, mine, other, rotated, frames, atoms, scale)


def body(sizes, node_features, frames, radial, neighbours, counts, coefficients, *weights):
    atoms_here, _, channels = node_features.shape
    slots = neighbours.shape[1]
    edges = atoms_here * slots
    most = edges // TILE
    devices = int(np.prod(list(sizes.values())))
    n_narrow = sizes["z"] * sizes["yh"]
    n_xy = sizes["x"] * sizes["yl"]

    narrow = lax.axis_index(NARROW)
    rows = np.array([BLOCKS[min(g, len(BLOCKS) - 1)] for g in range(n_narrow * BLOCKS_EACH)], np.int32)
    table = lax.dynamic_slice_in_dim(jnp.asarray(rows), narrow * BLOCKS_EACH, BLOCKS_EACH, 0)
    partial = combine(table, coefficients, weights)
    share_rows = partial.shape[1] // n_xy
    parts = lax.all_to_all(partial.reshape(-1, share_rows, C), ("core", "x", "yl"), 0, 0, tiled=True)
    share = jnp.sum(parts.astype(jnp.float32), axis=0).astype(jnp.bfloat16)
    copies = jnp.broadcast_to(share[None], (n_narrow * n_xy,) + share.shape)
    mine = lax.all_to_all(copies, SAME_CORE, 0, 0, tiled=True).reshape(-1, C)

    block = lax.axis_index(ATOM_AXES)
    side = (neighbours // atoms_here - block) % devices
    local = neighbours % atoms_here + jnp.where(side == 0, 0, jnp.where(side == 1, 2 * atoms_here, atoms_here))
    before = np.tril(np.ones((atoms_here, atoms_here), np.int32), -1)
    offset = jnp.sum(before * counts[None, :], axis=1)
    ends = offset + counts
    slot = lax.broadcasted_iota(jnp.int32, (atoms_here, slots), 1)
    position = jnp.where(slot < counts[:, None], offset[:, None] + slot, -1).reshape(edges // C, 1, C)
    places = jnp.arange(edges, dtype=jnp.int32)
    atoms = jnp.sum((ends[None, :] <= places[:, None]).astype(jnp.int32), axis=1)
    starts = jnp.arange(most, dtype=jnp.int32) * TILE
    first_atom = jnp.sum((ends[None, :] <= starts[:, None]).astype(jnp.int32), axis=1)
    first = jnp.minimum(first_atom * slots // C, (edges - WINDOW) // C)
    tiles = ((jnp.sum(counts) + TILE - 1) // TILE).astype(jnp.int32).reshape(1)

    own, first, position, _ = lax.optimization_barrier((node_features.transpose(1, 0, 2), first, position, partial))
    turned, factor = compact(
        tiles, first, position, local.reshape(position.shape), frames.reshape(edges, -1), radial.reshape(edges, C)
    )
    up = [(i, (i + 1) % devices) for i in range(devices)]
    low = lax.ppermute(own, ATOM_AXES, up)
    high = lax.ppermute(own, ATOM_AXES, [(b, a) for a, b in up])
    turned, low, high = lax.optimization_barrier((turned, low, high))
    rotated = rotate(tiles, turned, factor, own, low, high)
    mine, rotated, turned = lax.optimization_barrier((mine, rotated, turned))
    other = lax.ppermute(mine, "core", [(0, 1), (1, 0)])
    scale = jnp.broadcast_to(1.0 / jnp.sqrt(counts.astype(jnp.float32))[:, None], (atoms_here, C))
    info = jnp.concatenate([lax.axis_index("core").astype(jnp.int32).reshape(1), tiles])
    out = mix(info, mine, other, rotated, turned, atoms.reshape(most, 1, TILE), scale)
    return out.transpose(1, 0, 2)


def solution(mesh):
    sizes = {"x": mesh.shape["wide"] // 4, "yl": 2, "core": 2, "z": mesh.shape["narrow"] // 2, "yh": 2}
    fine = Mesh(mesh.devices.reshape(tuple(sizes.values())), tuple(sizes))
    in_specs = (
        P(ATOM_AXES, None, None),
        P(ATOM_AXES, None, None),
        P(ATOM_AXES, None, None),
        P(ATOM_AXES, None),
        P(ATOM_AXES),
        P(WIDE),
        P(WIDE, None, None),
        P(WIDE, None, None, None),
        P(WIDE, None, None, None),
        P(WIDE, None, None, None),
        P(WIDE, None, None, None),
    )
    out_specs = P(ATOM_AXES, None, None)
    return jax.shard_map(functools.partial(body, sizes), mesh=fine, in_specs=in_specs, out_specs=out_specs, check_vma=False)
```

```python
import functools

import jax
import jax.numpy as jnp
import numpy as np
from jax import lax
from jax.experimental import pallas as pl
from jax.experimental.pallas import tpu as pltpu
from jax.sharding import Mesh, PartitionSpec as P

WIDE = ("x", "yl", "core")
NARROW = ("z", "yh")
ATOM_AXES = WIDE + NARROW
SAME_CORE = ("z", "yh", "x", "yl")
C = 128
TILE = 256
STRIP = 32
WINDOW = 1024
BLOCKS_EACH = 11
INDEX_LANE = 165
DEPTH = (5, 8, 6, 4, 2)
START = (0, 5, 13, 19, 23)
VMEM = 100 * 2**20 // 2


def grouped_place():
    place = {}
    at = 0
    for degree in range(5):
        place[degree * degree + degree] = at
        at += 1
    for order in range(1, 5):
        for sign in (1, -1):
            for degree in range(order, 5):
                place[degree * degree + degree + sign * order] = at
                at += 1
    return place


PLACE = grouped_place()


def block_list():
    blocks = [(0, 0, o, i) for o in range(5) for i in range(5)]
    for order in range(1, 5):
        kept = 5 - order
        blocks += [(order, part, o, i) for part in range(2) for o in range(kept) for i in range(kept)]
    return blocks


BLOCKS = block_list()


def combine_kernel(table, coeff, w0, w1, w2, w3, w4, out, buf, sems):
    arrays = (w0, w1, w2, w3, w4)
    mine = lax.axis_index("z") * lax.axis_size("yh") + lax.axis_index("yh")
    for j in range(BLOCKS_EACH):
        at = (mine * BLOCKS_EACH + j) * 4
        kind = table[at]
        part = table[at + 1]
        row = pl.multiple_of(table[at + 3] * C, C)
        column = pl.multiple_of(table[at + 2] * C, C)
        for a, ref in enumerate(arrays):

            @pl.when(kind == a)
            def _():
                if a == 0:
                    source = ref.at[:, pl.ds(row, C), pl.ds(column, C)]
                else:
                    source = ref.at[:, part, pl.ds(row, C), pl.ds(column, C)]
                pltpu.make_async_copy(source, buf.at[j], sems.at[j]).start()

    for j in range(BLOCKS_EACH):
        pltpu.make_async_copy(w0.at[:, pl.ds(0, C), pl.ds(0, C)], buf.at[j], sems.at[j]).wait()
        total = coeff[0] * buf[j, 0].astype(jnp.float32) + coeff[1] * buf[j, 1].astype(jnp.float32)
        turned = total.T.astype(jnp.bfloat16)
        out[0, 64 * j : 64 * j + 64] = turned[:64]
        out[1, 64 * j : 64 * j + 64] = turned[64:]


def combine(table, coeff, weights):
    return pl.pallas_call(
        combine_kernel,
        grid_spec=pltpu.PrefetchScalarGridSpec(
            num_scalar_prefetch=2,
            grid=(1,),
            in_specs=[pl.BlockSpec(memory_space=pltpu.HBM)] * 5,
            out_specs=pl.BlockSpec((2, 64 * BLOCKS_EACH, C), lambda i, *_: (0, 0, 0)),
            scratch_shapes=[
                pltpu.VMEM((BLOCKS_EACH, 2, C, C), jnp.bfloat16),
                pltpu.SemaphoreType.DMA((BLOCKS_EACH,)),
            ],
        ),
        out_shape=jax.ShapeDtypeStruct((2, 64 * BLOCKS_EACH, C), jnp.bfloat16),
        compiler_params=pltpu.CompilerParams(vmem_limit_bytes=62 * 2**20),
        cost_estimate=pl.CostEstimate(flops=BLOCKS_EACH * C * C * 4, bytes_accessed=BLOCKS_EACH * C * C * 6, transcendentals=0),
        name="merge_group",
    )(table, coeff, *weights)


def spread_frames(turned, spread):
    for k in range(INDEX_LANE):
        spread[k] = jnp.broadcast_to(turned[k : k + 1, :], (16, TILE)).astype(jnp.bfloat16)


def tree_sum(terms):
    while len(terms) > 1:
        terms = [terms[i] + terms[i + 1] if i + 1 < len(terms) else terms[i] for i in range(0, len(terms), 2)]
    return terms[0]


def compact_kernel(first, tiles, position, local, frames, radial, out_frames, out_radial):
    step = pl.program_id(0)

    @pl.when(step < tiles[0])
    def _():
        begin = first[step]
        edge = lax.broadcasted_iota(jnp.int32, (TILE, C), 0) + step * TILE
        chosen = jnp.concatenate(
            [(position[begin + j] == edge).astype(jnp.float32).astype(jnp.bfloat16) for j in range(WINDOW // C)], axis=1
        )
        window = pl.ds(pl.multiple_of(begin * C, C), WINDOW)
        packed = jnp.dot(chosen, frames[window, :], preferred_element_type=jnp.float32)
        out_frames[0, :INDEX_LANE] = packed.T
        index = jnp.concatenate([local[begin + j] for j in range(WINDOW // C)], axis=1)
        index = jnp.broadcast_to(index, (8, WINDOW)).astype(jnp.bfloat16)
        moved = lax.dot_general(index, chosen, (((1,), (1,)), ((), ())), preferred_element_type=jnp.float32)
        out_frames[0, INDEX_LANE : INDEX_LANE + 1] = moved[:1]
        out_radial[0] = jnp.dot(chosen, radial[window, :], preferred_element_type=jnp.float32).T


def compact(tiles, first, position, local, frames, radial):
    whole = lambda *shape: pl.BlockSpec(shape, lambda i, *_: (0,) * len(shape))
    most = frames.shape[0] // TILE
    tile = lambda rows: pl.BlockSpec((1, rows, TILE), lambda i, f, n: (jnp.minimum(i, n[0] - 1), 0, 0))
    return pl.pallas_call(
        compact_kernel,
        grid_spec=pltpu.PrefetchScalarGridSpec(
            num_scalar_prefetch=2,
            grid=(most,),
            in_specs=[whole(*a.shape) for a in (position, local, frames, radial)],
            out_specs=[tile(168), tile(C)],
        ),
        out_shape=[
            jax.ShapeDtypeStruct((most, 168, TILE), jnp.float32),
            jax.ShapeDtypeStruct((most, C, TILE), jnp.float32),
        ],
        compiler_params=pltpu.CompilerParams(vmem_limit_bytes=VMEM),
        cost_estimate=pl.CostEstimate(flops=2 * 10**10, bytes_accessed=40 * 10**6, transcendentals=0),
        name="compact_edges",
    )(first, tiles, position, local, frames, radial)


def rotate_kernel(tiles, frames, radial, own, low, high, out, table, gathered, spread):
    step = pl.program_id(0)

    @pl.when(step == 0)
    def _():
        for q in range(25):
            rows = jnp.concatenate([own[q], low[q], high[q]], axis=0)
            table[q * C : (q + 1) * C, :] = rows.T

    @pl.when(step < tiles[0])
    def _():
        rotate_tile(frames, radial, out, table, gathered, spread)


def rotate_tile(frames, radial, out, table, gathered, spread):
    spread_frames(frames[0], spread)
    index = frames[0, INDEX_LANE : INDEX_LANE + 1, :].astype(jnp.int32)
    one_hot = (lax.broadcasted_iota(jnp.int32, (192, TILE), 0) == index).astype(jnp.float32).astype(jnp.bfloat16)
    offset = 0
    for degree in range(5):
        size = 2 * degree + 1
        base = degree * degree
        for q in range(base, base + size):
            rows = slice(q * C, (q + 1) * C)
            got = jnp.dot(table[rows, :], one_hot, preferred_element_type=jnp.float32)
            gathered[rows, :] = (got * radial[0]).astype(jnp.bfloat16)
        for at in range(0, C, STRIP):
            x = [[gathered[(base + q) * C + i : (base + q) * C + i + 16, :] for i in range(at, at + STRIP, 16)] for q in range(size)]
            for p in range(size):
                entries = [spread[offset + p * size + q] for q in range(size)]
                for k in range(STRIP // 16):
                    row = PLACE[base + p] * C + at + 16 * k
                    out[0, row : row + 16, :] = tree_sum([entries[q] * x[q][k] for q in range(size)])
        offset += size * size


def rotate(tiles, frames, radial, own, low, high):
    whole = lambda *shape: pl.BlockSpec(shape, lambda i, *_: (0,) * len(shape))
    most = frames.shape[0]
    tile = lambda rows: pl.BlockSpec((1, rows, TILE), lambda i, n: (jnp.minimum(i, n[0] - 1), 0, 0))
    return pl.pallas_call(
        rotate_kernel,
        grid_spec=pltpu.PrefetchScalarGridSpec(
            num_scalar_prefetch=1,
            grid=(most,),
            in_specs=[tile(168), tile(C)] + [whole(*own.shape)] * 3,
            out_specs=tile(25 * C),
            scratch_shapes=[
                pltpu.VMEM((25 * C, 192), jnp.bfloat16),
                pltpu.VMEM((25 * C, TILE), jnp.bfloat16),
                pltpu.VMEM((INDEX_LANE, 16, TILE), jnp.bfloat16),
            ],
        ),
        out_shape=jax.ShapeDtypeStruct((most, 25 * C, TILE), jnp.bfloat16),
        compiler_params=pltpu.CompilerParams(vmem_limit_bytes=VMEM),
        cost_estimate=pl.CostEstimate(flops=10**10, bytes_accessed=40 * 10**6, transcendentals=0),
        name="gather_rotate",
    )(tiles, frames, radial, own, low, high)


def place_weights(core, mine, other, mixes):
    for g, (order, part, o, i) in enumerate(BLOCKS):
        kept = C * DEPTH[order] // 2
        for half, ref in ((core, mine), (1 - core, other)):
            piece = ref[64 * g : 64 * g + 64, :]
            shift = half * 64

            def put(row, column, value):
                mixes[order][pl.ds(pl.multiple_of(row + shift, 64), 64), column : column + C] = value

            if order == 0:
                put(o * C, i * C, piece)
            elif part == 0:
                put(o * C, i * C, piece)
                put(kept + o * C, kept + i * C, piece)
            else:
                put(kept + o * C, i * C, piece)
                put(o * C, kept + i * C, -piece)


def mix_kernel(info, mine, other, rotated, frames, bounds, scale, out, m0, m1, m2, m3, m4, fresh, gated, message, spread, total):
    step = pl.program_id(0)
    mixes = (m0, m1, m2, m3, m4)

    @pl.when(step == 0)
    def _():
        place_weights(info[0], mine, other, mixes)
        total[...] = jnp.zeros_like(total)
        gated[...] = jnp.zeros_like(gated)

    @pl.when(step <= info[1])
    def _():
        mix_tile(step, rotated, frames, bounds, mixes, fresh, gated, message, spread, total)

    @pl.when(step == info[1])
    def _():
        for q in range(25):
            out[q] = total[q * C : (q + 1) * C, :].T * scale[...]


def mix_tile(step, rotated, frames, bounds, mixes, fresh, gated, message, spread, total):
    edge = lax.broadcasted_iota(jnp.int32, (TILE, 64), 0) + (step - 1) * TILE
    owned = jnp.logical_and(edge >= bounds[0:1, :], edge < bounds[1:2, :])
    owner = owned.astype(jnp.float32).astype(jnp.bfloat16)
    spread_frames(frames[0], spread)

    def mix_order(order, gate):
        begin = START[order] * C
        size = DEPTH[order]
        mixed = jnp.dot(mixes[order][...], rotated[0, begin : begin + size * C], preferred_element_type=jnp.float32)
        if order == 0:
            gate = 1.0 / (1.0 + jnp.exp(-mixed[:C]))
        for k in range(size):
            fresh[begin + k * C : begin + (k + 1) * C] = (mixed[k * C : (k + 1) * C] * gate).astype(jnp.bfloat16)
        return gate

    def turn_back(degree):
        size = 2 * degree + 1
        base = degree * degree
        offset = sum((2 * d + 1) ** 2 for d in range(degree))
        for at in range(0, C, STRIP):
            g = [
                [gated[PLACE[base + p] * C + i : PLACE[base + p] * C + i + 16, :] for i in range(at, at + STRIP, 16)]
                for p in range(size)
            ]
            for q in range(size):
                entries = [spread[offset + p * size + q] for p in range(size)]
                for k in range(STRIP // 16):
                    row = (base + q) * C + at + 16 * k
                    message[row : row + 16, :] = tree_sum([entries[p] * g[p][k] for p in range(size)])
        rows = slice(base * C, (base + size) * C)
        total[rows, :] += jnp.dot(message[rows, :], owner, preferred_element_type=jnp.float32)

    gate = mix_order(0, None)
    turn_back(4)
    mix_order(1, gate)
    turn_back(3)
    mix_order(2, gate)
    turn_back(2)
    mix_order(3, gate)
    turn_back(1)
    mix_order(4, gate)
    turn_back(0)
    gated[...] = fresh[...]


def mix(info, mine, other, rotated, frames, bounds, scale):
    whole = lambda *shape: pl.BlockSpec(shape, lambda i, *_: (0,) * len(shape))
    block = lambda a, lag: pl.BlockSpec((1,) + a.shape[1:], lambda i, n: (jnp.clip(i - lag, 0, n[1] - 1), 0, 0))
    return pl.pallas_call(
        mix_kernel,
        grid_spec=pltpu.PrefetchScalarGridSpec(
            num_scalar_prefetch=1,
            grid=(rotated.shape[0] + 1,),
            in_specs=[
                whole(*mine.shape),
                whole(*other.shape),
                block(rotated, 0),
                block(frames, 1),
                whole(*bounds.shape),
                whole(*scale.shape),
            ],
            out_specs=whole(25, 64, C),
            scratch_shapes=[pltpu.VMEM((d * C, d * C), jnp.bfloat16) for d in DEPTH]
            + [
                pltpu.VMEM((25 * C, TILE), jnp.bfloat16),
                pltpu.VMEM((25 * C, TILE), jnp.bfloat16),
                pltpu.VMEM((25 * C, TILE), jnp.bfloat16),
                pltpu.VMEM((INDEX_LANE, 16, TILE), jnp.bfloat16),
                pltpu.VMEM((25 * C, 64), jnp.float32),
            ],
        ),
        out_shape=jax.ShapeDtypeStruct((25, 64, C), jnp.float32),
        compiler_params=pltpu.CompilerParams(vmem_limit_bytes=VMEM),
        cost_estimate=pl.CostEstimate(flops=15 * 10**9, bytes_accessed=40 * 10**6, transcendentals=10**6),
        name="mix_messages",
    )(info, mine, other, rotated, frames, bounds, scale)


def body(sizes, node_features, frames, radial, neighbours, counts, coefficients, *weights):
    atoms_here, _, channels = node_features.shape
    slots = neighbours.shape[1]
    edges = atoms_here * slots
    most = edges // TILE
    devices = int(np.prod(list(sizes.values())))
    n_narrow = sizes["z"] * sizes["yh"]
    n_xy = sizes["x"] * sizes["yl"]

    rows = np.array([BLOCKS[min(g, len(BLOCKS) - 1)] for g in range(n_narrow * BLOCKS_EACH)], np.int32)
    partial = combine(jnp.asarray(rows.reshape(-1)), coefficients, weights)
    share_rows = partial.shape[1] // n_xy
    parts = lax.all_to_all(partial.reshape(-1, share_rows, C), ("core", "x", "yl"), 0, 0, tiled=True)
    share = jnp.sum(parts.astype(jnp.float32), axis=0).astype(jnp.bfloat16)
    copies = jnp.broadcast_to(share[None], (n_narrow * n_xy,) + share.shape)
    mine = lax.all_to_all(copies, SAME_CORE, 0, 0, tiled=True).reshape(-1, C)

    block = lax.axis_index(ATOM_AXES)
    side = (neighbours // atoms_here - block) % devices
    local = neighbours % atoms_here + jnp.where(side == 0, 0, jnp.where(side == 1, 2 * atoms_here, atoms_here))
    before = np.tril(np.ones((atoms_here, atoms_here), np.int32), -1)
    offset = jnp.sum(before * counts[None, :], axis=1)
    ends = offset + counts
    slot = lax.broadcasted_iota(jnp.int32, (atoms_here, slots), 1)
    position = jnp.where(slot < counts[:, None], offset[:, None] + slot, -1).reshape(edges // C, 1, C)
    starts = jnp.arange(most, dtype=jnp.int32) * TILE
    first_atom = jnp.sum((ends[None, :] <= starts[:, None]).astype(jnp.int32), axis=1)
    first = jnp.minimum(first_atom * slots // C, (edges - WINDOW) // C)
    tiles = ((jnp.sum(counts) + TILE - 1) // TILE).astype(jnp.int32).reshape(1)

    own, first, position, _ = lax.optimization_barrier((node_features.transpose(1, 0, 2), first, position, partial))
    turned, factor = compact(
        tiles, first, position, local.reshape(position.shape), frames.reshape(edges, -1), radial.reshape(edges, C)
    )
    up = [(i, (i + 1) % devices) for i in range(devices)]
    low = lax.ppermute(own, ATOM_AXES, up)
    high = lax.ppermute(own, ATOM_AXES, [(b, a) for a, b in up])
    turned, low, high = lax.optimization_barrier((turned, low, high))
    rotated = rotate(tiles, turned, factor, own, low, high)
    mine, rotated, turned = lax.optimization_barrier((mine, rotated, turned))
    other = lax.ppermute(mine, "core", [(0, 1), (1, 0)])
    scale = jnp.broadcast_to(1.0 / jnp.sqrt(counts.astype(jnp.float32))[:, None], (atoms_here, C))
    info = jnp.concatenate([lax.axis_index("core").astype(jnp.int32).reshape(1), tiles])
    out = mix(info, mine, other, rotated, turned, jnp.stack([offset, ends]), scale)
    return out.transpose(1, 0, 2)


def solution(mesh):
    sizes = {"x": mesh.shape["wide"] // 4, "yl": 2, "core": 2, "z": mesh.shape["narrow"] // 2, "yh": 2}
    fine = Mesh(mesh.devices.reshape(tuple(sizes.values())), tuple(sizes))
    in_specs = (
        P(ATOM_AXES, None, None),
        P(ATOM_AXES, None, None),
        P(ATOM_AXES, None, None),
        P(ATOM_AXES, None),
        P(ATOM_AXES),
        P(WIDE),
        P(WIDE, None, None),
        P(WIDE, None, None, None),
        P(WIDE, None, None, None),
        P(WIDE, None, None, None),
        P(WIDE, None, None, None),
    )
    out_specs = P(ATOM_AXES, None, None)
    return jax.shard_map(functools.partial(body, sizes), mesh=fine, in_specs=in_specs, out_specs=out_specs, check_vma=False)
```

```python
import functools

import jax
import jax.numpy as jnp
import numpy as np
from jax import lax
from jax.experimental import pallas as pl
from jax.experimental.pallas import tpu as pltpu
from jax.sharding import Mesh, PartitionSpec as P

WIDE = ("x", "yl", "core")
NARROW = ("z", "yh")
ATOM_AXES = WIDE + NARROW
SAME_CORE = ("z", "yh", "x", "yl")
C = 128
TILE = 256
STRIP = 32
WINDOW = 1024
BLOCKS_EACH = 11
INDEX_LANE = 165
DEPTH = (5, 8, 6, 4, 2)
START = (0, 5, 13, 19, 23)
THREE = (1, 3)
VMEM = 100 * 2**20 // 2


def grouped_place():
    place = {}
    at = 0
    for degree in range(5):
        place[degree * degree + degree] = at
        at += 1
    for order in range(1, 5):
        for sign in (1, -1):
            for degree in range(order, 5):
                place[degree * degree + degree + sign * order] = at
                at += 1
    return place


PLACE = grouped_place()


def block_list():
    blocks = [(0, 0, o, i) for o in range(5) for i in range(5)]
    for order in range(1, 5):
        kept = 5 - order
        blocks += [(order, part, o, i) for part in range(2) for o in range(kept) for i in range(kept)]
    return blocks


BLOCKS = block_list()


def combine_kernel(table, coeff, w0, w1, w2, w3, w4, out, buf, sems):
    arrays = (w0, w1, w2, w3, w4)
    mine = lax.axis_index("z") * lax.axis_size("yh") + lax.axis_index("yh")
    for j in range(BLOCKS_EACH):
        at = (mine * BLOCKS_EACH + j) * 4
        kind = table[at]
        part = table[at + 1]
        row = pl.multiple_of(table[at + 3] * C, C)
        column = pl.multiple_of(table[at + 2] * C, C)
        for a, ref in enumerate(arrays):

            @pl.when(kind == a)
            def _():
                if a == 0:
                    source = ref.at[:, pl.ds(row, C), pl.ds(column, C)]
                else:
                    source = ref.at[:, part, pl.ds(row, C), pl.ds(column, C)]
                pltpu.make_async_copy(source, buf.at[j], sems.at[j]).start()

    for j in range(BLOCKS_EACH):
        pltpu.make_async_copy(w0.at[:, pl.ds(0, C), pl.ds(0, C)], buf.at[j], sems.at[j]).wait()
        total = coeff[0] * buf[j, 0].astype(jnp.float32) + coeff[1] * buf[j, 1].astype(jnp.float32)
        turned = total.T.astype(jnp.bfloat16)
        out[0, 64 * j : 64 * j + 64] = turned[:64]
        out[1, 64 * j : 64 * j + 64] = turned[64:]


def combine(table, coeff, weights):
    return pl.pallas_call(
        combine_kernel,
        grid_spec=pltpu.PrefetchScalarGridSpec(
            num_scalar_prefetch=2,
            grid=(1,),
            in_specs=[pl.BlockSpec(memory_space=pltpu.HBM)] * 5,
            out_specs=pl.BlockSpec((2, 64 * BLOCKS_EACH, C), lambda i, *_: (0, 0, 0)),
            scratch_shapes=[
                pltpu.VMEM((BLOCKS_EACH, 2, C, C), jnp.bfloat16),
                pltpu.SemaphoreType.DMA((BLOCKS_EACH,)),
            ],
        ),
        out_shape=jax.ShapeDtypeStruct((2, 64 * BLOCKS_EACH, C), jnp.bfloat16),
        compiler_params=pltpu.CompilerParams(vmem_limit_bytes=62 * 2**20),
        cost_estimate=pl.CostEstimate(flops=BLOCKS_EACH * C * C * 4, bytes_accessed=BLOCKS_EACH * C * C * 6, transcendentals=0),
        name="merge_group",
    )(table, coeff, *weights)


def spread_frames(turned, spread):
    for k in range(INDEX_LANE):
        spread[k] = jnp.broadcast_to(turned[k : k + 1, :], (16, TILE)).astype(jnp.bfloat16)


def tree_sum(terms):
    while len(terms) > 1:
        terms = [terms[i] + terms[i + 1] if i + 1 < len(terms) else terms[i] for i in range(0, len(terms), 2)]
    return terms[0]


def compact_kernel(first, tiles, position, local, frames, radial, out_frames, out_radial):
    step = pl.program_id(0)

    @pl.when(step < tiles[0])
    def _():
        begin = first[step]
        edge = lax.broadcasted_iota(jnp.int32, (TILE, C), 0) + step * TILE
        chosen = jnp.concatenate(
            [(position[begin + j] == edge).astype(jnp.float32).astype(jnp.bfloat16) for j in range(WINDOW // C)], axis=1
        )
        window = pl.ds(pl.multiple_of(begin * C, C), WINDOW)
        packed = jnp.dot(chosen, frames[window, :], preferred_element_type=jnp.float32)
        out_frames[0, :INDEX_LANE] = packed.T
        index = jnp.concatenate([local[begin + j] for j in range(WINDOW // C)], axis=1)
        index = jnp.broadcast_to(index, (8, WINDOW)).astype(jnp.bfloat16)
        moved = lax.dot_general(index, chosen, (((1,), (1,)), ((), ())), preferred_element_type=jnp.float32)
        out_frames[0, INDEX_LANE : INDEX_LANE + 1] = moved[:1]
        out_radial[0] = jnp.dot(chosen, radial[window, :], preferred_element_type=jnp.float32).T


def compact(tiles, first, position, local, frames, radial):
    whole = lambda *shape: pl.BlockSpec(shape, lambda i, *_: (0,) * len(shape))
    most = frames.shape[0] // TILE
    tile = lambda rows: pl.BlockSpec((1, rows, TILE), lambda i, f, n: (jnp.minimum(i, n[0] - 1), 0, 0))
    return pl.pallas_call(
        compact_kernel,
        grid_spec=pltpu.PrefetchScalarGridSpec(
            num_scalar_prefetch=2,
            grid=(most,),
            in_specs=[whole(*a.shape) for a in (position, local, frames, radial)],
            out_specs=[tile(168), tile(C)],
        ),
        out_shape=[
            jax.ShapeDtypeStruct((most, 168, TILE), jnp.float32),
            jax.ShapeDtypeStruct((most, C, TILE), jnp.float32),
        ],
        compiler_params=pltpu.CompilerParams(vmem_limit_bytes=VMEM),
        cost_estimate=pl.CostEstimate(flops=2 * 10**10, bytes_accessed=40 * 10**6, transcendentals=0),
        name="compact_edges",
    )(first, tiles, position, local, frames, radial)


def rotate_kernel(tiles, frames, radial, own, low, high, out, table, gathered, spread):
    step = pl.program_id(0)

    @pl.when(step == 0)
    def _():
        for q in range(25):
            rows = jnp.concatenate([own[q], low[q], high[q]], axis=0)
            table[q * C : (q + 1) * C, :] = rows.T

    @pl.when(step < tiles[0])
    def _():
        rotate_tile(frames, radial, out, table, gathered, spread)


def rotate_tile(frames, radial, out, table, gathered, spread):
    spread_frames(frames[0], spread)
    index = frames[0, INDEX_LANE : INDEX_LANE + 1, :].astype(jnp.int32)
    one_hot = (lax.broadcasted_iota(jnp.int32, (192, TILE), 0) == index).astype(jnp.float32).astype(jnp.bfloat16)
    offset = 0
    for degree in range(5):
        size = 2 * degree + 1
        base = degree * degree
        for q in range(base, base + size):
            rows = slice(q * C, (q + 1) * C)
            got = jnp.dot(table[rows, :], one_hot, preferred_element_type=jnp.float32)
            gathered[rows, :] = (got * radial[0]).astype(jnp.bfloat16)
        for at in range(0, C, STRIP):
            x = [[gathered[(base + q) * C + i : (base + q) * C + i + 16, :] for i in range(at, at + STRIP, 16)] for q in range(size)]
            for p in range(size):
                entries = [spread[offset + p * size + q] for q in range(size)]
                for k in range(STRIP // 16):
                    row = PLACE[base + p] * C + at + 16 * k
                    out[0, row : row + 16, :] = tree_sum([entries[q] * x[q][k] for q in range(size)])
        offset += size * size


def rotate(tiles, frames, radial, own, low, high):
    whole = lambda *shape: pl.BlockSpec(shape, lambda i, *_: (0,) * len(shape))
    most = frames.shape[0]
    tile = lambda rows: pl.BlockSpec((1, rows, TILE), lambda i, n: (jnp.minimum(i, n[0] - 1), 0, 0))
    return pl.pallas_call(
        rotate_kernel,
        grid_spec=pltpu.PrefetchScalarGridSpec(
            num_scalar_prefetch=1,
            grid=(most,),
            in_specs=[tile(168), tile(C)] + [whole(*own.shape)] * 3,
            out_specs=tile(25 * C),
            scratch_shapes=[
                pltpu.VMEM((25 * C, 192), jnp.bfloat16),
                pltpu.VMEM((25 * C, TILE), jnp.bfloat16),
                pltpu.VMEM((INDEX_LANE, 16, TILE), jnp.bfloat16),
            ],
        ),
        out_shape=jax.ShapeDtypeStruct((most, 25 * C, TILE), jnp.bfloat16),
        compiler_params=pltpu.CompilerParams(vmem_limit_bytes=VMEM),
        cost_estimate=pl.CostEstimate(flops=10**10, bytes_accessed=40 * 10**6, transcendentals=0),
        name="gather_rotate",
    )(tiles, frames, radial, own, low, high)


def mix_shape(order):
    size = DEPTH[order] * C
    return (3, size // 2, size // 2) if order in THREE else (size, size)


def place_weights(core, mine, other, mixes):
    where = {block: g for g, block in enumerate(BLOCKS)}
    for g, (order, part, o, i) in enumerate(BLOCKS):
        if order in THREE:
            if part == 0:
                pair = where[order, 1, o, i]
                for half, ref in ((core, mine), (1 - core, other)):
                    real = ref[64 * g : 64 * g + 64, :]
                    imag = ref[64 * pair : 64 * pair + 64, :]
                    wide_real = real.astype(jnp.float32)
                    wide_imag = imag.astype(jnp.float32)
                    rows = pl.ds(pl.multiple_of(o * C + half * 64, 64), 64)
                    columns = slice(i * C, (i + 1) * C)
                    mixes[order][0, rows, columns] = real
                    mixes[order][1, rows, columns] = (wide_imag - wide_real).astype(jnp.bfloat16)
                    mixes[order][2, rows, columns] = (wide_real + wide_imag).astype(jnp.bfloat16)
            continue
        kept = C * DEPTH[order] // 2
        for half, ref in ((core, mine), (1 - core, other)):
            piece = ref[64 * g : 64 * g + 64, :]
            shift = half * 64

            def put(row, column, value):
                mixes[order][pl.ds(pl.multiple_of(row + shift, 64), 64), column : column + C] = value

            if order == 0:
                put(o * C, i * C, piece)
            elif part == 0:
                put(o * C, i * C, piece)
                put(kept + o * C, kept + i * C, piece)
            else:
                put(kept + o * C, i * C, piece)
                put(o * C, kept + i * C, -piece)


def mix_kernel(info, mine, other, rotated, frames, bounds, scale, out, m0, m1, m2, m3, m4, fresh, gated, message, spread, total):
    step = pl.program_id(0)
    mixes = (m0, m1, m2, m3, m4)

    @pl.when(step == 0)
    def _():
        place_weights(info[0], mine, other, mixes)
        total[...] = jnp.zeros_like(total)
        gated[...] = jnp.zeros_like(gated)

    @pl.when(step <= info[1])
    def _():
        mix_tile(step, rotated, frames, bounds, mixes, fresh, gated, message, spread, total)

    @pl.when(step == info[1])
    def _():
        for q in range(25):
            out[q] = total[q * C : (q + 1) * C, :].T * scale[...]


def mix_tile(step, rotated, frames, bounds, mixes, fresh, gated, message, spread, total):
    edge = lax.broadcasted_iota(jnp.int32, (TILE, 64), 0) + (step - 1) * TILE
    owned = jnp.logical_and(edge >= bounds[0:1, :], edge < bounds[1:2, :])
    owner = owned.astype(jnp.float32).astype(jnp.bfloat16)
    spread_frames(frames[0], spread)

    def mix_order(order, gate):
        begin = START[order] * C
        size = DEPTH[order]
        if order in THREE:
            half = size * C // 2
            plus = rotated[0, begin : begin + half]
            minus = rotated[0, begin + half : begin + size * C]
            dot = lambda k, x: jnp.dot(mixes[order][k], x, preferred_element_type=jnp.float32)
            shared = dot(0, plus + minus)
            up = shared - dot(2, minus)
            for k in range(size // 2):
                fresh[begin + k * C : begin + (k + 1) * C] = (up[k * C : (k + 1) * C] * gate).astype(jnp.bfloat16)
            down = shared + dot(1, plus)
            for k in range(size // 2):
                at = begin + half + k * C
                fresh[at : at + C] = (down[k * C : (k + 1) * C] * gate).astype(jnp.bfloat16)
            return gate
        mixed = jnp.dot(mixes[order][...], rotated[0, begin : begin + size * C], preferred_element_type=jnp.float32)
        if order == 0:
            gate = 1.0 / (1.0 + jnp.exp(-mixed[:C]))
        for k in range(size):
            fresh[begin + k * C : begin + (k + 1) * C] = (mixed[k * C : (k + 1) * C] * gate).astype(jnp.bfloat16)
        return gate

    def turn_back(degree):
        size = 2 * degree + 1
        base = degree * degree
        offset = sum((2 * d + 1) ** 2 for d in range(degree))
        for at in range(0, C, STRIP):
            g = [
                [gated[PLACE[base + p] * C + i : PLACE[base + p] * C + i + 16, :] for i in range(at, at + STRIP, 16)]
                for p in range(size)
            ]
            for q in range(size):
                entries = [spread[offset + p * size + q] for p in range(size)]
                for k in range(STRIP // 16):
                    row = (base + q) * C + at + 16 * k
                    message[row : row + 16, :] = tree_sum([entries[p] * g[p][k] for p in range(size)])
        rows = slice(base * C, (base + size) * C)
        total[rows, :] += jnp.dot(message[rows, :], owner, preferred_element_type=jnp.float32)

    gate = mix_order(0, None)
    turn_back(4)
    mix_order(1, gate)
    turn_back(3)
    mix_order(2, gate)
    turn_back(2)
    mix_order(3, gate)
    turn_back(1)
    mix_order(4, gate)
    turn_back(0)
    gated[...] = fresh[...]


def mix(info, mine, other, rotated, frames, bounds, scale):
    whole = lambda *shape: pl.BlockSpec(shape, lambda i, *_: (0,) * len(shape))
    block = lambda a, lag: pl.BlockSpec((1,) + a.shape[1:], lambda i, n: (jnp.clip(i - lag, 0, n[1] - 1), 0, 0))
    return pl.pallas_call(
        mix_kernel,
        grid_spec=pltpu.PrefetchScalarGridSpec(
            num_scalar_prefetch=1,
            grid=(rotated.shape[0] + 1,),
            in_specs=[
                whole(*mine.shape),
                whole(*other.shape),
                block(rotated, 0),
                block(frames, 1),
                whole(*bounds.shape),
                whole(*scale.shape),
            ],
            out_specs=whole(25, 64, C),
            scratch_shapes=[pltpu.VMEM(mix_shape(order), jnp.bfloat16) for order in range(5)]
            + [
                pltpu.VMEM((25 * C, TILE), jnp.bfloat16),
                pltpu.VMEM((25 * C, TILE), jnp.bfloat16),
                pltpu.VMEM((25 * C, TILE), jnp.bfloat16),
                pltpu.VMEM((INDEX_LANE, 16, TILE), jnp.bfloat16),
                pltpu.VMEM((25 * C, 64), jnp.float32),
            ],
        ),
        out_shape=jax.ShapeDtypeStruct((25, 64, C), jnp.float32),
        compiler_params=pltpu.CompilerParams(vmem_limit_bytes=VMEM),
        cost_estimate=pl.CostEstimate(flops=15 * 10**9, bytes_accessed=40 * 10**6, transcendentals=10**6),
        name="mix_messages",
    )(info, mine, other, rotated, frames, bounds, scale)


def body(sizes, node_features, frames, radial, neighbours, counts, coefficients, *weights):
    atoms_here, _, channels = node_features.shape
    slots = neighbours.shape[1]
    edges = atoms_here * slots
    most = edges // TILE
    devices = int(np.prod(list(sizes.values())))
    n_narrow = sizes["z"] * sizes["yh"]
    n_xy = sizes["x"] * sizes["yl"]

    rows = np.array([BLOCKS[min(g, len(BLOCKS) - 1)] for g in range(n_narrow * BLOCKS_EACH)], np.int32)
    partial = combine(jnp.asarray(rows.reshape(-1)), coefficients, weights)
    share_rows = partial.shape[1] // n_xy
    parts = lax.all_to_all(partial.reshape(-1, share_rows, C), ("core", "x", "yl"), 0, 0, tiled=True)
    share = jnp.sum(parts.astype(jnp.float32), axis=0).astype(jnp.bfloat16)
    copies = jnp.broadcast_to(share[None], (n_narrow * n_xy,) + share.shape)
    mine = lax.all_to_all(copies, SAME_CORE, 0, 0, tiled=True).reshape(-1, C)

    block = lax.axis_index(ATOM_AXES)
    side = (neighbours // atoms_here - block) % devices
    local = neighbours % atoms_here + jnp.where(side == 0, 0, jnp.where(side == 1, 2 * atoms_here, atoms_here))
    before = np.tril(np.ones((atoms_here, atoms_here), np.int32), -1)
    offset = jnp.sum(before * counts[None, :], axis=1)
    ends = offset + counts
    slot = lax.broadcasted_iota(jnp.int32, (atoms_here, slots), 1)
    position = jnp.where(slot < counts[:, None], offset[:, None] + slot, -1).reshape(edges // C, 1, C)
    starts = jnp.arange(most, dtype=jnp.int32) * TILE
    first_atom = jnp.sum((ends[None, :] <= starts[:, None]).astype(jnp.int32), axis=1)
    first = jnp.minimum(first_atom * slots // C, (edges - WINDOW) // C)
    tiles = ((jnp.sum(counts) + TILE - 1) // TILE).astype(jnp.int32).reshape(1)

    own, first, position, _ = lax.optimization_barrier((node_features.transpose(1, 0, 2), first, position, partial))
    turned, factor = compact(
        tiles, first, position, local.reshape(position.shape), frames.reshape(edges, -1), radial.reshape(edges, C)
    )
    up = [(i, (i + 1) % devices) for i in range(devices)]
    low = lax.ppermute(own, ATOM_AXES, up)
    high = lax.ppermute(node_features.transpose(1, 0, 2), ATOM_AXES, [(b, a) for a, b in up])
    turned, low, high = lax.optimization_barrier((turned, low, high))
    rotated = rotate(tiles, turned, factor, own, low, high)
    mine, rotated, turned = lax.optimization_barrier((mine, rotated, turned))
    other = lax.ppermute(mine, "core", [(0, 1), (1, 0)])
    scale = jnp.broadcast_to(1.0 / jnp.sqrt(counts.astype(jnp.float32))[:, None], (atoms_here, C))
    info = jnp.concatenate([lax.axis_index("core").astype(jnp.int32).reshape(1), tiles])
    out = mix(info, mine, other, rotated, turned, jnp.stack([offset, ends]), scale)
    return out.transpose(1, 0, 2)


def solution(mesh):
    sizes = {"x": mesh.shape["wide"] // 4, "yl": 2, "core": 2, "z": mesh.shape["narrow"] // 2, "yh": 2}
    fine = Mesh(mesh.devices.reshape(tuple(sizes.values())), tuple(sizes))
    in_specs = (
        P(ATOM_AXES, None, None),
        P(ATOM_AXES, None, None),
        P(ATOM_AXES, None, None),
        P(ATOM_AXES, None),
        P(ATOM_AXES),
        P(WIDE),
        P(WIDE, None, None),
        P(WIDE, None, None, None),
        P(WIDE, None, None, None),
        P(WIDE, None, None, None),
        P(WIDE, None, None, None),
    )
    out_specs = P(ATOM_AXES, None, None)
    return jax.shard_map(functools.partial(body, sizes), mesh=fine, in_specs=in_specs, out_specs=out_specs, check_vma=False)
```

```python
import functools

import jax
import jax.numpy as jnp
import numpy as np
from jax import lax
from jax.experimental import pallas as pl
from jax.experimental.pallas import tpu as pltpu
from jax.sharding import Mesh, PartitionSpec as P

WIDE = ("x", "yl", "core")
NARROW = ("z", "yh")
ATOM_AXES = WIDE + NARROW
SAME_CORE = ("z", "yh", "x", "yl")
C = 128
TILE = 256
STRIP = 32
WINDOW = 1024
BLOCKS_EACH = 11
INDEX_LANE = 165
DEPTH = (5, 8, 6, 4, 2)
START = (0, 5, 13, 19, 23)
THREE = (1, 3)
VMEM = 100 * 2**20 // 2


def grouped_place():
    place = {}
    at = 0
    for degree in range(5):
        place[degree * degree + degree] = at
        at += 1
    for order in range(1, 5):
        for sign in (1, -1):
            for degree in range(order, 5):
                place[degree * degree + degree + sign * order] = at
                at += 1
    return place


PLACE = grouped_place()


def block_list():
    blocks = [(0, 0, o, i) for o in range(5) for i in range(5)]
    for order in range(1, 5):
        kept = 5 - order
        blocks += [(order, part, o, i) for part in range(2) for o in range(kept) for i in range(kept)]
    return blocks


BLOCKS = block_list()


def combine_kernel(table, coeff, w0, w1, w2, w3, w4, out, buf, sems):
    arrays = (w0, w1, w2, w3, w4)
    mine = lax.axis_index("z") * lax.axis_size("yh") + lax.axis_index("yh")
    for j in range(BLOCKS_EACH):
        at = (mine * BLOCKS_EACH + j) * 4
        kind = table[at]
        part = table[at + 1]
        row = pl.multiple_of(table[at + 3] * C, C)
        column = pl.multiple_of(table[at + 2] * C, C)
        for a, ref in enumerate(arrays):

            @pl.when(kind == a)
            def _():
                if a == 0:
                    source = ref.at[:, pl.ds(row, C), pl.ds(column, C)]
                else:
                    source = ref.at[:, part, pl.ds(row, C), pl.ds(column, C)]
                pltpu.make_async_copy(source, buf.at[j], sems.at[j]).start()

    for j in range(BLOCKS_EACH):
        pltpu.make_async_copy(w0.at[:, pl.ds(0, C), pl.ds(0, C)], buf.at[j], sems.at[j]).wait()
        total = coeff[0] * buf[j, 0].astype(jnp.float32) + coeff[1] * buf[j, 1].astype(jnp.float32)
        turned = total.T.astype(jnp.bfloat16)
        out[0, 64 * j : 64 * j + 64] = turned[:64]
        out[1, 64 * j : 64 * j + 64] = turned[64:]


def combine(table, coeff, weights):
    return pl.pallas_call(
        combine_kernel,
        grid_spec=pltpu.PrefetchScalarGridSpec(
            num_scalar_prefetch=2,
            grid=(1,),
            in_specs=[pl.BlockSpec(memory_space=pltpu.HBM)] * 5,
            out_specs=pl.BlockSpec((2, 64 * BLOCKS_EACH, C), lambda i, *_: (0, 0, 0)),
            scratch_shapes=[
                pltpu.VMEM((BLOCKS_EACH, 2, C, C), jnp.bfloat16),
                pltpu.SemaphoreType.DMA((BLOCKS_EACH,)),
            ],
        ),
        out_shape=jax.ShapeDtypeStruct((2, 64 * BLOCKS_EACH, C), jnp.bfloat16),
        compiler_params=pltpu.CompilerParams(vmem_limit_bytes=62 * 2**20),
        cost_estimate=pl.CostEstimate(flops=BLOCKS_EACH * C * C * 4, bytes_accessed=BLOCKS_EACH * C * C * 6, transcendentals=0),
        name="merge_group",
    )(table, coeff, *weights)


def spread_frames(turned, spread):
    for k in range(INDEX_LANE):
        spread[k] = jnp.broadcast_to(turned[k : k + 1, :], (16, TILE)).astype(jnp.bfloat16)


def tree_sum(terms):
    while len(terms) > 1:
        terms = [terms[i] + terms[i + 1] if i + 1 < len(terms) else terms[i] for i in range(0, len(terms), 2)]
    return terms[0]


def compact_kernel(first, tiles, position, local, frames, radial, out_frames, out_radial):
    step = pl.program_id(0)

    @pl.when(step < tiles[0])
    def _():
        begin = first[step]
        edge = lax.broadcasted_iota(jnp.int32, (TILE, C), 0) + step * TILE
        chosen = jnp.concatenate(
            [(position[begin + j] == edge).astype(jnp.float32).astype(jnp.bfloat16) for j in range(WINDOW // C)], axis=1
        )
        window = pl.ds(pl.multiple_of(begin * C, C), WINDOW)
        packed = jnp.dot(chosen, frames[window, :], preferred_element_type=jnp.float32)
        out_frames[0, :INDEX_LANE] = packed.T
        index = jnp.concatenate([local[begin + j] for j in range(WINDOW // C)], axis=1)
        index = jnp.broadcast_to(index, (8, WINDOW)).astype(jnp.bfloat16)
        moved = lax.dot_general(index, chosen, (((1,), (1,)), ((), ())), preferred_element_type=jnp.float32)
        out_frames[0, INDEX_LANE : INDEX_LANE + 1] = moved[:1]
        out_radial[0] = jnp.dot(chosen, radial[window, :], preferred_element_type=jnp.float32).T


def compact(tiles, first, position, local, frames, radial):
    whole = lambda *shape: pl.BlockSpec(shape, lambda i, *_: (0,) * len(shape))
    most = frames.shape[0] // TILE
    tile = lambda rows: pl.BlockSpec((1, rows, TILE), lambda i, f, n: (jnp.minimum(i, n[0] - 1), 0, 0))
    return pl.pallas_call(
        compact_kernel,
        grid_spec=pltpu.PrefetchScalarGridSpec(
            num_scalar_prefetch=2,
            grid=(most,),
            in_specs=[whole(*a.shape) for a in (position, local, frames, radial)],
            out_specs=[tile(168), tile(C)],
        ),
        out_shape=[
            jax.ShapeDtypeStruct((most, 168, TILE), jnp.float32),
            jax.ShapeDtypeStruct((most, C, TILE), jnp.float32),
        ],
        compiler_params=pltpu.CompilerParams(vmem_limit_bytes=VMEM),
        cost_estimate=pl.CostEstimate(flops=2 * 10**10, bytes_accessed=40 * 10**6, transcendentals=0),
        name="compact_edges",
    )(first, tiles, position, local, frames, radial)


def rotate_kernel(tiles, frames, radial, own, low, high, out, table, gathered, spread):
    step = pl.program_id(0)

    @pl.when(step == 0)
    def _():
        for q in range(25):
            rows = jnp.concatenate([own[q], low[q], high[q]], axis=0)
            table[q * C : (q + 1) * C, :] = rows.T

    @pl.when(step < tiles[0])
    def _():
        rotate_tile(frames, radial, out, table, gathered, spread)


def rotate_tile(frames, radial, out, table, gathered, spread):
    spread_frames(frames[0], spread)
    index = frames[0, INDEX_LANE : INDEX_LANE + 1, :].astype(jnp.int32)
    one_hot = (lax.broadcasted_iota(jnp.int32, (192, TILE), 0) == index).astype(jnp.float32).astype(jnp.bfloat16)
    offset = 0
    for degree in range(5):
        size = 2 * degree + 1
        base = degree * degree
        for q in range(base, base + size):
            rows = slice(q * C, (q + 1) * C)
            got = jnp.dot(table[rows, :], one_hot, preferred_element_type=jnp.float32)
            gathered[rows, :] = (got * radial[0]).astype(jnp.bfloat16)
        for at in range(0, C, STRIP):
            x = [[gathered[(base + q) * C + i : (base + q) * C + i + 16, :] for i in range(at, at + STRIP, 16)] for q in range(size)]
            for p in range(size):
                entries = [spread[offset + p * size + q] for q in range(size)]
                for k in range(STRIP // 16):
                    row = PLACE[base + p] * C + at + 16 * k
                    out[0, row : row + 16, :] = tree_sum([entries[q] * x[q][k] for q in range(size)])
        offset += size * size


def rotate(tiles, frames, radial, own, low, high):
    whole = lambda *shape: pl.BlockSpec(shape, lambda i, *_: (0,) * len(shape))
    most = frames.shape[0]
    tile = lambda rows: pl.BlockSpec((1, rows, TILE), lambda i, n: (jnp.minimum(i, n[0] - 1), 0, 0))
    return pl.pallas_call(
        rotate_kernel,
        grid_spec=pltpu.PrefetchScalarGridSpec(
            num_scalar_prefetch=1,
            grid=(most,),
            in_specs=[tile(168), tile(C)] + [whole(*own.shape)] * 3,
            out_specs=tile(25 * C),
            scratch_shapes=[
                pltpu.VMEM((25 * C, 192), jnp.bfloat16),
                pltpu.VMEM((25 * C, TILE), jnp.bfloat16),
                pltpu.VMEM((INDEX_LANE, 16, TILE), jnp.bfloat16),
            ],
        ),
        out_shape=jax.ShapeDtypeStruct((most, 25 * C, TILE), jnp.bfloat16),
        compiler_params=pltpu.CompilerParams(vmem_limit_bytes=VMEM),
        cost_estimate=pl.CostEstimate(flops=10**10, bytes_accessed=40 * 10**6, transcendentals=0),
        name="gather_rotate",
    )(tiles, frames, radial, own, low, high)


def mix_shape(order):
    size = DEPTH[order] * C
    return (3, size // 2, size // 2) if order in THREE else (size, size)


def place_weights(core, mine, other, mixes):
    where = {block: g for g, block in enumerate(BLOCKS)}
    for g, (order, part, o, i) in enumerate(BLOCKS):
        if order in THREE:
            if part == 0:
                pair = where[order, 1, o, i]
                for half, ref in ((core, mine), (1 - core, other)):
                    real = ref[64 * g : 64 * g + 64, :]
                    imag = ref[64 * pair : 64 * pair + 64, :]
                    wide_real = real.astype(jnp.float32)
                    wide_imag = imag.astype(jnp.float32)
                    rows = pl.ds(pl.multiple_of(o * C + half * 64, 64), 64)
                    columns = slice(i * C, (i + 1) * C)
                    mixes[order][0, rows, columns] = real
                    mixes[order][1, rows, columns] = (wide_imag - wide_real).astype(jnp.bfloat16)
                    mixes[order][2, rows, columns] = (wide_real + wide_imag).astype(jnp.bfloat16)
            continue
        kept = C * DEPTH[order] // 2
        for half, ref in ((core, mine), (1 - core, other)):
            piece = ref[64 * g : 64 * g + 64, :]
            shift = half * 64

            def put(row, column, value):
                mixes[order][pl.ds(pl.multiple_of(row + shift, 64), 64), column : column + C] = value

            if order == 0:
                put(o * C, i * C, piece)
            elif part == 0:
                put(o * C, i * C, piece)
                put(kept + o * C, kept + i * C, piece)
            else:
                put(kept + o * C, i * C, piece)
                put(o * C, kept + i * C, -piece)


def mix_kernel(info, mine, other, rotated, frames, bounds, scale, out, m0, m1, m2, m3, m4, fresh, gated, message, spread, total):
    step = pl.program_id(0)
    mixes = (m0, m1, m2, m3, m4)

    @pl.when(step == 0)
    def _():
        place_weights(info[0], mine, other, mixes)
        total[...] = jnp.zeros_like(total)

    refs = (step, rotated, frames, bounds, mixes, fresh, gated, message, spread, total)

    @pl.when(step == 0)
    def _():
        mix_tile(True, False, *refs)

    @pl.when(jnp.logical_and(step > 0, step < info[1]))
    def _():
        mix_tile(True, True, *refs)

    @pl.when(step == info[1])
    def _():
        mix_tile(False, True, *refs)

    @pl.when(step == info[1])
    def _():
        for q in range(25):
            out[q] = total[q * C : (q + 1) * C, :].T * scale[...]


def mix_tile(mixing, turning, step, rotated, frames, bounds, mixes, fresh, gated, message, spread, total):
    edge = lax.broadcasted_iota(jnp.int32, (TILE, 64), 0) + (step - 1) * TILE
    owned = jnp.logical_and(edge >= bounds[0:1, :], edge < bounds[1:2, :])
    owner = owned.astype(jnp.float32).astype(jnp.bfloat16)
    if turning:
        spread_frames(frames[0], spread)

    def mix_order(order, gate):
        begin = START[order] * C
        size = DEPTH[order]
        if order in THREE:
            half = size * C // 2
            plus = rotated[0, begin : begin + half]
            minus = rotated[0, begin + half : begin + size * C]
            dot = lambda k, x: jnp.dot(mixes[order][k], x, preferred_element_type=jnp.float32)
            shared = dot(0, plus + minus)
            up = shared - dot(2, minus)
            for k in range(size // 2):
                fresh[begin + k * C : begin + (k + 1) * C] = (up[k * C : (k + 1) * C] * gate).astype(jnp.bfloat16)
            down = shared + dot(1, plus)
            for k in range(size // 2):
                at = begin + half + k * C
                fresh[at : at + C] = (down[k * C : (k + 1) * C] * gate).astype(jnp.bfloat16)
            return gate
        mixed = jnp.dot(mixes[order][...], rotated[0, begin : begin + size * C], preferred_element_type=jnp.float32)
        if order == 0:
            gate = 1.0 / (1.0 + jnp.exp(-mixed[:C]))
        for k in range(size):
            fresh[begin + k * C : begin + (k + 1) * C] = (mixed[k * C : (k + 1) * C] * gate).astype(jnp.bfloat16)
        return gate

    def turn_back(degree):
        size = 2 * degree + 1
        base = degree * degree
        offset = sum((2 * d + 1) ** 2 for d in range(degree))
        for at in range(0, C, STRIP):
            g = [
                [gated[PLACE[base + p] * C + i : PLACE[base + p] * C + i + 16, :] for i in range(at, at + STRIP, 16)]
                for p in range(size)
            ]
            for q in range(size):
                entries = [spread[offset + p * size + q] for p in range(size)]
                for k in range(STRIP // 16):
                    row = (base + q) * C + at + 16 * k
                    message[row : row + 16, :] = tree_sum([entries[p] * g[p][k] for p in range(size)])
        rows = slice(base * C, (base + size) * C)
        total[rows, :] += jnp.dot(message[rows, :], owner, preferred_element_type=jnp.float32)

    gate = mix_order(0, None) if mixing else None
    for degree, order in ((4, 1), (3, 2), (2, 3), (1, 4), (0, None)):
        if turning:
            turn_back(degree)
        if mixing and order:
            mix_order(order, gate)
    if mixing:
        gated[...] = fresh[...]


def mix(info, mine, other, rotated, frames, bounds, scale):
    whole = lambda *shape: pl.BlockSpec(shape, lambda i, *_: (0,) * len(shape))
    block = lambda a, lag: pl.BlockSpec((1,) + a.shape[1:], lambda i, n: (jnp.clip(i - lag, 0, n[1] - 1), 0, 0))
    return pl.pallas_call(
        mix_kernel,
        grid_spec=pltpu.PrefetchScalarGridSpec(
            num_scalar_prefetch=1,
            grid=(rotated.shape[0] + 1,),
            in_specs=[
                whole(*mine.shape),
                whole(*other.shape),
                block(rotated, 0),
                block(frames, 1),
                whole(*bounds.shape),
                whole(*scale.shape),
            ],
            out_specs=whole(25, 64, C),
            scratch_shapes=[pltpu.VMEM(mix_shape(order), jnp.bfloat16) for order in range(5)]
            + [
                pltpu.VMEM((25 * C, TILE), jnp.bfloat16),
                pltpu.VMEM((25 * C, TILE), jnp.bfloat16),
                pltpu.VMEM((25 * C, TILE), jnp.bfloat16),
                pltpu.VMEM((INDEX_LANE, 16, TILE), jnp.bfloat16),
                pltpu.VMEM((25 * C, 64), jnp.float32),
            ],
        ),
        out_shape=jax.ShapeDtypeStruct((25, 64, C), jnp.float32),
        compiler_params=pltpu.CompilerParams(vmem_limit_bytes=VMEM),
        cost_estimate=pl.CostEstimate(flops=15 * 10**9, bytes_accessed=40 * 10**6, transcendentals=10**6),
        name="mix_messages",
    )(info, mine, other, rotated, frames, bounds, scale)


def body(sizes, node_features, frames, radial, neighbours, counts, coefficients, *weights):
    atoms_here, _, channels = node_features.shape
    slots = neighbours.shape[1]
    edges = atoms_here * slots
    most = edges // TILE
    devices = int(np.prod(list(sizes.values())))
    n_narrow = sizes["z"] * sizes["yh"]
    n_xy = sizes["x"] * sizes["yl"]

    rows = np.array([BLOCKS[min(g, len(BLOCKS) - 1)] for g in range(n_narrow * BLOCKS_EACH)], np.int32)
    partial = combine(jnp.asarray(rows.reshape(-1)), coefficients, weights)
    share_rows = partial.shape[1] // n_xy
    parts = lax.all_to_all(partial.reshape(-1, share_rows, C), ("core", "x", "yl"), 0, 0, tiled=True)
    share = jnp.sum(parts.astype(jnp.float32), axis=0).astype(jnp.bfloat16)
    copies = jnp.broadcast_to(share[None], (n_narrow * n_xy,) + share.shape)
    mine = lax.all_to_all(copies, SAME_CORE, 0, 0, tiled=True).reshape(-1, C)

    block = lax.axis_index(ATOM_AXES)
    side = (neighbours // atoms_here - block) % devices
    local = neighbours % atoms_here + jnp.where(side == 0, 0, jnp.where(side == 1, 2 * atoms_here, atoms_here))
    before = np.tril(np.ones((atoms_here, atoms_here), np.int32), -1)
    offset = jnp.sum(before * counts[None, :], axis=1)
    ends = offset + counts
    slot = lax.broadcasted_iota(jnp.int32, (atoms_here, slots), 1)
    position = jnp.where(slot < counts[:, None], offset[:, None] + slot, -1).reshape(edges // C, 1, C)
    starts = jnp.arange(most, dtype=jnp.int32) * TILE
    first_atom = jnp.sum((ends[None, :] <= starts[:, None]).astype(jnp.int32), axis=1)
    first = jnp.minimum(first_atom * slots // C, (edges - WINDOW) // C)
    tiles = ((jnp.sum(counts) + TILE - 1) // TILE).astype(jnp.int32).reshape(1)

    own, first, position, _ = lax.optimization_barrier((node_features.transpose(1, 0, 2), first, position, partial))
    turned, factor = compact(
        tiles, first, position, local.reshape(position.shape), frames.reshape(edges, -1), radial.reshape(edges, C)
    )
    up = [(i, (i + 1) % devices) for i in range(devices)]
    low = lax.ppermute(own, ATOM_AXES, up)
    high = lax.ppermute(node_features.transpose(1, 0, 2), ATOM_AXES, [(b, a) for a, b in up])
    turned, low, high = lax.optimization_barrier((turned, low, high))
    rotated = rotate(tiles, turned, factor, own, low, high)
    mine, rotated, turned = lax.optimization_barrier((mine, rotated, turned))
    other = lax.ppermute(mine, "core", [(0, 1), (1, 0)])
    scale = jnp.broadcast_to(1.0 / jnp.sqrt(counts.astype(jnp.float32))[:, None], (atoms_here, C))
    info = jnp.concatenate([lax.axis_index("core").astype(jnp.int32).reshape(1), tiles])
    out = mix(info, mine, other, rotated, turned, jnp.stack([offset, ends]), scale)
    return out.transpose(1, 0, 2)


def solution(mesh):
    sizes = {"x": mesh.shape["wide"] // 4, "yl": 2, "core": 2, "z": mesh.shape["narrow"] // 2, "yh": 2}
    fine = Mesh(mesh.devices.reshape(tuple(sizes.values())), tuple(sizes))
    in_specs = (
        P(ATOM_AXES, None, None),
        P(ATOM_AXES, None, None),
        P(ATOM_AXES, None, None),
        P(ATOM_AXES, None),
        P(ATOM_AXES),
        P(WIDE),
        P(WIDE, None, None),
        P(WIDE, None, None, None),
        P(WIDE, None, None, None),
        P(WIDE, None, None, None),
        P(WIDE, None, None, None),
    )
    out_specs = P(ATOM_AXES, None, None)
    return jax.shard_map(functools.partial(body, sizes), mesh=fine, in_specs=in_specs, out_specs=out_specs, check_vma=False)
```

```python
import functools

import jax
import jax.numpy as jnp
import numpy as np
from jax import lax
from jax.experimental import pallas as pl
from jax.experimental.pallas import tpu as pltpu
from jax.sharding import Mesh, PartitionSpec as P

WIDE = ("x", "yl", "core")
NARROW = ("z", "yh")
ATOM_AXES = WIDE + NARROW
SAME_CORE = ("z", "yh", "x", "yl")
C = 128
TILE = 256
STRIP = 32
WINDOW = 1024
BLOCKS_EACH = 11
INDEX_LANE = 165
DEPTH = (5, 8, 6, 4, 2)
START = (0, 5, 13, 19, 23)
THREE = (1, 3)
VMEM = 100 * 2**20 // 2


def grouped_place():
    place = {}
    at = 0
    for degree in range(5):
        place[degree * degree + degree] = at
        at += 1
    for order in range(1, 5):
        for sign in (1, -1):
            for degree in range(order, 5):
                place[degree * degree + degree + sign * order] = at
                at += 1
    return place


PLACE = grouped_place()


def block_list():
    blocks = [(0, 0, o, i) for o in range(5) for i in range(5)]
    for order in range(1, 5):
        kept = 5 - order
        blocks += [(order, part, o, i) for part in range(2) for o in range(kept) for i in range(kept)]
    return blocks


BLOCKS = block_list()


def combine_kernel(table, coeff, w0, w1, w2, w3, w4, out, buf, sems):
    arrays = (w0, w1, w2, w3, w4)
    mine = lax.axis_index("z") * lax.axis_size("yh") + lax.axis_index("yh")
    for j in range(BLOCKS_EACH):
        at = (mine * BLOCKS_EACH + j) * 4
        kind = table[at]
        part = table[at + 1]
        row = pl.multiple_of(table[at + 3] * C, C)
        column = pl.multiple_of(table[at + 2] * C, C)
        for a, ref in enumerate(arrays):

            @pl.when(kind == a)
            def _():
                if a == 0:
                    source = ref.at[:, pl.ds(row, C), pl.ds(column, C)]
                else:
                    source = ref.at[:, part, pl.ds(row, C), pl.ds(column, C)]
                pltpu.make_async_copy(source, buf.at[j], sems.at[j]).start()

    for j in range(BLOCKS_EACH):
        pltpu.make_async_copy(w0.at[:, pl.ds(0, C), pl.ds(0, C)], buf.at[j], sems.at[j]).wait()
        total = coeff[0] * buf[j, 0].astype(jnp.float32) + coeff[1] * buf[j, 1].astype(jnp.float32)
        turned = total.astype(jnp.bfloat16).T
        out[0, 64 * j : 64 * j + 64] = turned[:64]
        out[1, 64 * j : 64 * j + 64] = turned[64:]


def combine(table, coeff, weights):
    return pl.pallas_call(
        combine_kernel,
        grid_spec=pltpu.PrefetchScalarGridSpec(
            num_scalar_prefetch=2,
            grid=(1,),
            in_specs=[pl.BlockSpec(memory_space=pltpu.HBM)] * 5,
            out_specs=pl.BlockSpec((2, 64 * BLOCKS_EACH, C), lambda i, *_: (0, 0, 0)),
            scratch_shapes=[
                pltpu.VMEM((BLOCKS_EACH, 2, C, C), jnp.bfloat16),
                pltpu.SemaphoreType.DMA((BLOCKS_EACH,)),
            ],
        ),
        out_shape=jax.ShapeDtypeStruct((2, 64 * BLOCKS_EACH, C), jnp.bfloat16),
        compiler_params=pltpu.CompilerParams(vmem_limit_bytes=62 * 2**20),
        cost_estimate=pl.CostEstimate(flops=BLOCKS_EACH * C * C * 4, bytes_accessed=BLOCKS_EACH * C * C * 6, transcendentals=0),
        name="merge_group",
    )(table, coeff, *weights)


def spread_frames(turned, spread):
    for k in range(INDEX_LANE):
        spread[k] = jnp.broadcast_to(turned[k : k + 1, :], (16, TILE)).astype(jnp.bfloat16)


def tree_sum(terms):
    while len(terms) > 1:
        terms = [terms[i] + terms[i + 1] if i + 1 < len(terms) else terms[i] for i in range(0, len(terms), 2)]
    return terms[0]


def compact_kernel(first, tiles, position, local, frames, radial, out_frames, out_radial):
    step = pl.program_id(0)

    @pl.when(step < tiles[0])
    def _():
        begin = first[step]
        edge = lax.broadcasted_iota(jnp.int32, (TILE, C), 0) + step * TILE
        chosen = jnp.concatenate(
            [(position[begin + j] == edge).astype(jnp.float32).astype(jnp.bfloat16) for j in range(WINDOW // C)], axis=1
        )
        window = pl.ds(pl.multiple_of(begin * C, C), WINDOW)
        packed = jnp.dot(chosen, frames[window, :], preferred_element_type=jnp.float32)
        out_frames[0, :INDEX_LANE] = packed.T
        index = jnp.concatenate([local[begin + j] for j in range(WINDOW // C)], axis=1)
        index = jnp.broadcast_to(index, (8, WINDOW)).astype(jnp.bfloat16)
        moved = lax.dot_general(index, chosen, (((1,), (1,)), ((), ())), preferred_element_type=jnp.float32)
        out_frames[0, INDEX_LANE : INDEX_LANE + 1] = moved[:1]
        out_radial[0] = jnp.dot(chosen, radial[window, :], preferred_element_type=jnp.float32).T


def compact(tiles, first, position, local, frames, radial):
    whole = lambda *shape: pl.BlockSpec(shape, lambda i, *_: (0,) * len(shape))
    most = frames.shape[0] // TILE
    tile = lambda rows: pl.BlockSpec((1, rows, TILE), lambda i, f, n: (jnp.minimum(i, n[0] - 1), 0, 0))
    return pl.pallas_call(
        compact_kernel,
        grid_spec=pltpu.PrefetchScalarGridSpec(
            num_scalar_prefetch=2,
            grid=(most,),
            in_specs=[whole(*a.shape) for a in (position, local, frames, radial)],
            out_specs=[tile(168), tile(C)],
        ),
        out_shape=[
            jax.ShapeDtypeStruct((most, 168, TILE), jnp.float32),
            jax.ShapeDtypeStruct((most, C, TILE), jnp.float32),
        ],
        compiler_params=pltpu.CompilerParams(vmem_limit_bytes=VMEM),
        cost_estimate=pl.CostEstimate(flops=2 * 10**10, bytes_accessed=40 * 10**6, transcendentals=0),
        name="compact_edges",
    )(first, tiles, position, local, frames, radial)


def rotate_kernel(tiles, frames, radial, own, low, high, out, table, gathered, spread):
    step = pl.program_id(0)

    @pl.when(step == 0)
    def _():
        for q in range(25):
            rows = jnp.concatenate([own[q], low[q], high[q]], axis=0)
            table[q * C : (q + 1) * C, :] = rows.T

    @pl.when(step < tiles[0])
    def _():
        rotate_tile(frames, radial, out, table, gathered, spread)


def rotate_tile(frames, radial, out, table, gathered, spread):
    spread_frames(frames[0], spread)
    index = frames[0, INDEX_LANE : INDEX_LANE + 1, :].astype(jnp.int32)
    one_hot = (lax.broadcasted_iota(jnp.int32, (192, TILE), 0) == index).astype(jnp.float32).astype(jnp.bfloat16)
    offset = 0
    for degree in range(5):
        size = 2 * degree + 1
        base = degree * degree
        for q in range(base, base + size):
            rows = slice(q * C, (q + 1) * C)
            got = jnp.dot(table[rows, :], one_hot, preferred_element_type=jnp.float32)
            gathered[rows, :] = (got * radial[0]).astype(jnp.bfloat16)
        for at in range(0, C, STRIP):
            x = [[gathered[(base + q) * C + i : (base + q) * C + i + 16, :] for i in range(at, at + STRIP, 16)] for q in range(size)]
            for p in range(size):
                entries = [spread[offset + p * size + q] for q in range(size)]
                for k in range(STRIP // 16):
                    row = PLACE[base + p] * C + at + 16 * k
                    out[0, row : row + 16, :] = tree_sum([entries[q] * x[q][k] for q in range(size)])
        offset += size * size


def rotate(tiles, frames, radial, own, low, high):
    whole = lambda *shape: pl.BlockSpec(shape, lambda i, *_: (0,) * len(shape))
    most = frames.shape[0]
    tile = lambda rows: pl.BlockSpec((1, rows, TILE), lambda i, n: (jnp.minimum(i, n[0] - 1), 0, 0))
    return pl.pallas_call(
        rotate_kernel,
        grid_spec=pltpu.PrefetchScalarGridSpec(
            num_scalar_prefetch=1,
            grid=(most,),
            in_specs=[tile(168), tile(C)] + [whole(*own.shape)] * 3,
            out_specs=tile(25 * C),
            scratch_shapes=[
                pltpu.VMEM((25 * C, 192), jnp.bfloat16),
                pltpu.VMEM((25 * C, TILE), jnp.bfloat16),
                pltpu.VMEM((INDEX_LANE, 16, TILE), jnp.bfloat16),
            ],
        ),
        out_shape=jax.ShapeDtypeStruct((most, 25 * C, TILE), jnp.bfloat16),
        compiler_params=pltpu.CompilerParams(vmem_limit_bytes=VMEM),
        cost_estimate=pl.CostEstimate(flops=10**10, bytes_accessed=40 * 10**6, transcendentals=0),
        name="gather_rotate",
    )(tiles, frames, radial, own, low, high)


def mix_shape(order):
    size = DEPTH[order] * C
    return (3, size // 2, size // 2) if order in THREE else (size, size)


def place_weights(which, core, mine, other, mixes):
    where = {block: g for g, block in enumerate(BLOCKS)}
    for g, (order, part, o, i) in enumerate(BLOCKS):
        if order != which:
            continue
        if order in THREE:
            if part == 0:
                pair = where[order, 1, o, i]
                for half, ref in ((core, mine), (1 - core, other)):
                    real = ref[64 * g : 64 * g + 64, :]
                    imag = ref[64 * pair : 64 * pair + 64, :]
                    wide_real = real.astype(jnp.float32)
                    wide_imag = imag.astype(jnp.float32)
                    rows = pl.ds(pl.multiple_of(o * C + half * 64, 64), 64)
                    columns = slice(i * C, (i + 1) * C)
                    mixes[order][0, rows, columns] = real
                    mixes[order][1, rows, columns] = (wide_imag - wide_real).astype(jnp.bfloat16)
                    mixes[order][2, rows, columns] = (wide_real + wide_imag).astype(jnp.bfloat16)
            continue
        kept = C * DEPTH[order] // 2
        for half, ref in ((core, mine), (1 - core, other)):
            piece = ref[64 * g : 64 * g + 64, :]
            shift = half * 64

            def put(row, column, value):
                mixes[order][pl.ds(pl.multiple_of(row + shift, 64), 64), column : column + C] = value

            if order == 0:
                put(o * C, i * C, piece)
            elif part == 0:
                put(o * C, i * C, piece)
                put(kept + o * C, kept + i * C, piece)
            else:
                put(kept + o * C, i * C, piece)
                put(o * C, kept + i * C, -piece)


def mix_kernel(info, mine, other, rotated, frames, bounds, scale, out, m0, m1, m2, m3, m4, fresh, gated, message, spread, total):
    step = pl.program_id(0)
    mixes = (m0, m1, m2, m3, m4)

    @pl.when(step == 0)
    def _():
        total[...] = jnp.zeros_like(total)

    refs = (step, rotated, frames, bounds, mixes, fresh, gated, message, spread, total)

    place = lambda order: place_weights(order, info[0], mine, other, mixes)

    @pl.when(step == 0)
    def _():
        mix_tile(place, True, False, *refs)

    @pl.when(jnp.logical_and(step > 0, step < info[1]))
    def _():
        mix_tile(None, True, True, *refs)

    @pl.when(step == info[1])
    def _():
        mix_tile(None, False, True, *refs)

    @pl.when(step == info[1])
    def _():
        for q in range(25):
            out[q] = total[q * C : (q + 1) * C, :].T * scale[...]


def mix_tile(place, mixing, turning, step, rotated, frames, bounds, mixes, fresh, gated, message, spread, total):
    edge = lax.broadcasted_iota(jnp.int32, (TILE, 64), 0) + (step - 1) * TILE
    owned = jnp.logical_and(edge >= bounds[0:1, :], edge < bounds[1:2, :])
    owner = owned.astype(jnp.float32).astype(jnp.bfloat16)
    if turning:
        spread_frames(frames[0], spread)

    def mix_order(order, gate):
        begin = START[order] * C
        size = DEPTH[order]
        if order in THREE:
            half = size * C // 2
            plus = rotated[0, begin : begin + half]
            minus = rotated[0, begin + half : begin + size * C]
            dot = lambda k, x: jnp.dot(mixes[order][k], x, preferred_element_type=jnp.float32)
            shared = dot(0, plus + minus)
            up = shared - dot(2, minus)
            for k in range(size // 2):
                fresh[begin + k * C : begin + (k + 1) * C] = (up[k * C : (k + 1) * C] * gate).astype(jnp.bfloat16)
            down = shared + dot(1, plus)
            for k in range(size // 2):
                at = begin + half + k * C
                fresh[at : at + C] = (down[k * C : (k + 1) * C] * gate).astype(jnp.bfloat16)
            return gate
        mixed = jnp.dot(mixes[order][...], rotated[0, begin : begin + size * C], preferred_element_type=jnp.float32)
        if order == 0:
            gate = 1.0 / (1.0 + jnp.exp(-mixed[:C]))
        for k in range(size):
            fresh[begin + k * C : begin + (k + 1) * C] = (mixed[k * C : (k + 1) * C] * gate).astype(jnp.bfloat16)
        return gate

    def turn_back(degree):
        size = 2 * degree + 1
        base = degree * degree
        offset = sum((2 * d + 1) ** 2 for d in range(degree))
        for at in range(0, C, STRIP):
            g = [
                [gated[PLACE[base + p] * C + i : PLACE[base + p] * C + i + 16, :] for i in range(at, at + STRIP, 16)]
                for p in range(size)
            ]
            for q in range(size):
                entries = [spread[offset + p * size + q] for p in range(size)]
                for k in range(STRIP // 16):
                    row = (base + q) * C + at + 16 * k
                    message[row : row + 16, :] = tree_sum([entries[p] * g[p][k] for p in range(size)])
        rows = slice(base * C, (base + size) * C)
        total[rows, :] += jnp.dot(message[rows, :], owner, preferred_element_type=jnp.float32)

    if place:
        place(0)
        place(1)
    gate = mix_order(0, None) if mixing else None
    for degree, order in ((4, 1), (3, 2), (2, 3), (1, 4), (0, None)):
        if turning:
            turn_back(degree)
        if place and order and order < 4:
            place(order + 1)
        if mixing and order:
            mix_order(order, gate)
    if mixing:
        gated[...] = fresh[...]


def mix(info, mine, other, rotated, frames, bounds, scale):
    whole = lambda *shape: pl.BlockSpec(shape, lambda i, *_: (0,) * len(shape))
    block = lambda a, lag: pl.BlockSpec((1,) + a.shape[1:], lambda i, n: (jnp.clip(i - lag, 0, n[1] - 1), 0, 0))
    return pl.pallas_call(
        mix_kernel,
        grid_spec=pltpu.PrefetchScalarGridSpec(
            num_scalar_prefetch=1,
            grid=(rotated.shape[0] + 1,),
            in_specs=[
                whole(*mine.shape),
                whole(*other.shape),
                block(rotated, 0),
                block(frames, 1),
                whole(*bounds.shape),
                whole(*scale.shape),
            ],
            out_specs=whole(25, 64, C),
            scratch_shapes=[pltpu.VMEM(mix_shape(order), jnp.bfloat16) for order in range(5)]
            + [
                pltpu.VMEM((25 * C, TILE), jnp.bfloat16),
                pltpu.VMEM((25 * C, TILE), jnp.bfloat16),
                pltpu.VMEM((25 * C, TILE), jnp.bfloat16),
                pltpu.VMEM((INDEX_LANE, 16, TILE), jnp.bfloat16),
                pltpu.VMEM((25 * C, 64), jnp.float32),
            ],
        ),
        out_shape=jax.ShapeDtypeStruct((25, 64, C), jnp.float32),
        compiler_params=pltpu.CompilerParams(vmem_limit_bytes=VMEM),
        cost_estimate=pl.CostEstimate(flops=15 * 10**9, bytes_accessed=40 * 10**6, transcendentals=10**6),
        name="mix_messages",
    )(info, mine, other, rotated, frames, bounds, scale)


def body(sizes, node_features, frames, radial, neighbours, counts, coefficients, *weights):
    atoms_here, _, channels = node_features.shape
    slots = neighbours.shape[1]
    edges = atoms_here * slots
    most = edges // TILE
    devices = int(np.prod(list(sizes.values())))
    n_narrow = sizes["z"] * sizes["yh"]
    n_xy = sizes["x"] * sizes["yl"]

    rows = np.array([BLOCKS[min(g, len(BLOCKS) - 1)] for g in range(n_narrow * BLOCKS_EACH)], np.int32)
    partial = combine(jnp.asarray(rows.reshape(-1)), coefficients, weights)
    share_rows = partial.shape[1] // n_xy
    parts = lax.all_to_all(partial.reshape(-1, share_rows, C), ("core", "x", "yl"), 0, 0, tiled=True)
    share = jnp.sum(parts.astype(jnp.float32), axis=0).astype(jnp.bfloat16)
    copies = jnp.broadcast_to(share[None], (n_narrow * n_xy,) + share.shape)
    mine = lax.all_to_all(copies, SAME_CORE, 0, 0, tiled=True).reshape(-1, C)

    block = lax.axis_index(ATOM_AXES)
    side = (neighbours // atoms_here - block) % devices
    local = neighbours % atoms_here + jnp.where(side == 0, 0, jnp.where(side == 1, 2 * atoms_here, atoms_here))
    before = np.tril(np.ones((atoms_here, atoms_here), np.int32), -1)
    offset = jnp.sum(before * counts[None, :], axis=1)
    ends = offset + counts
    slot = lax.broadcasted_iota(jnp.int32, (atoms_here, slots), 1)
    position = jnp.where(slot < counts[:, None], offset[:, None] + slot, -1).reshape(edges // C, 1, C)
    starts = jnp.arange(most, dtype=jnp.int32) * TILE
    first_atom = jnp.sum((ends[None, :] <= starts[:, None]).astype(jnp.int32), axis=1)
    first = jnp.minimum(first_atom * slots // C, (edges - WINDOW) // C)
    tiles = ((jnp.sum(counts) + TILE - 1) // TILE).astype(jnp.int32).reshape(1)

    own, first, position, _ = lax.optimization_barrier((node_features.transpose(1, 0, 2), first, position, partial))
    turned, factor = compact(
        tiles, first, position, local.reshape(position.shape), frames.reshape(edges, -1), radial.reshape(edges, C)
    )
    up = [(i, (i + 1) % devices) for i in range(devices)]
    low = lax.ppermute(own, ATOM_AXES, up)
    high = lax.ppermute(node_features.transpose(1, 0, 2), ATOM_AXES, [(b, a) for a, b in up])
    turned, low, high = lax.optimization_barrier((turned, low, high))
    rotated = rotate(tiles, turned, factor, own, low, high)
    mine, rotated, turned = lax.optimization_barrier((mine, rotated, turned))
    other = lax.ppermute(mine, "core", [(0, 1), (1, 0)])
    scale = jnp.broadcast_to(1.0 / jnp.sqrt(counts.astype(jnp.float32))[:, None], (atoms_here, C))
    info = jnp.concatenate([lax.axis_index("core").astype(jnp.int32).reshape(1), tiles])
    out = mix(info, mine, other, rotated, turned, jnp.stack([offset, ends]), scale)
    return out.transpose(1, 0, 2)


def solution(mesh):
    sizes = {"x": mesh.shape["wide"] // 4, "yl": 2, "core": 2, "z": mesh.shape["narrow"] // 2, "yh": 2}
    fine = Mesh(mesh.devices.reshape(tuple(sizes.values())), tuple(sizes))
    in_specs = (
        P(ATOM_AXES, None, None),
        P(ATOM_AXES, None, None),
        P(ATOM_AXES, None, None),
        P(ATOM_AXES, None),
        P(ATOM_AXES),
        P(WIDE),
        P(WIDE, None, None),
        P(WIDE, None, None, None),
        P(WIDE, None, None, None),
        P(WIDE, None, None, None),
        P(WIDE, None, None, None),
    )
    out_specs = P(ATOM_AXES, None, None)
    return jax.shard_map(functools.partial(body, sizes), mesh=fine, in_specs=in_specs, out_specs=out_specs, check_vma=False)
```
